32 devices in a mesh: dp: 8 (over z, y), mp: 4 (over x, core).
Axes of the slice: x: 2, y: 2, z: 4, core: 2. Of those that a mesh axis runs over, the one named last changes fastest.
Arguments:
- pixels: float32 [2048, 192], P('dp'), may hold values from -6 to 6
- variable_ids: int32 [8, 48], P('dp'), may hold values from 0 to 47, each once within a row
- variable_counts: int32 [8], P('dp'), may hold values from 8 to 48, as said below
- lead_hours: int32 [8], P('dp'), may hold values from 6 to 168
- dataset_ids: int32 [8], P('dp'), may hold values from 0 to 1
- patch_counts: int32 [8], P('dp'), may hold values from 85 to 256, as said below
- patch_weight: float32 [48, 4, 1024], replicated, may hold values from -3 to 3
- patch_bias: float32 [48, 1024], replicated, may hold values from -3 to 3
- variable_embed: float32 [48, 1024], replicated, may hold values from -3 to 3
- pool_query: float32 [2, 1024], replicated, may hold values from -6 to 6
- pool_in: float32 [3, 1024, 1024], P(None, None, 'mp'), may hold values from -0.1875 to 0.1875
- pool_out: float32 [1024, 1024], P('mp'), may hold values from -1 to 1
- position_embed: float32 [256, 1024], replicated, may hold values from -3 to 3
- lead_weight: float32 [1024], replicated, may hold values from -6 to 6
- lead_bias: float32 [1024], replicated, may hold values from -3 to 3
- first_gain: float32 [1024], replicated, may hold values from 0.1 to 1.9
- first_shift: float32 [1024], replicated, may hold values from -1.75 to 1.75
- attention_in: float32 [3, 1024, 1024], P(None, None, 'mp'), may hold values from -0.1875 to 0.1875
- attention_out: float32 [1024, 1024], P('mp'), may hold values from -2 to 2
- attention_bias: float32 [1024], replicated, may hold values from -1.75 to 1.75
- second_gain: float32 [1024], replicated, may hold values from 0.1 to 1.9
- second_shift: float32 [1024], replicated, may hold values from -1.75 to 1.75
- up_weight: float32 [1024, 4096], P(None, 'mp'), may hold values from -0.1875 to 0.1875
- up_bias: float32 [4096], P('mp'), may hold values from -3 to 3
- down_weight: float32 [4096, 1024], P('mp'), may hold values from -0.1875 to 0.1875
- down_bias: float32 [1024], replicated, may hold values from -1.75 to 1.75
- cotangent: float32 [2048, 1024], P('dp'), may hold values from -6 to 6
Outputs:
- block_output: float32 [2048, 1024], P('dp')
- pixels_grad: float32 [2048, 192], P('dp')
- patch_weight_grad: float32 [48, 4, 1024], replicated
- patch_bias_grad: float32 [48, 1024], replicated
- variable_embed_grad: float32 [48, 1024], replicated
- pool_query_grad: float32 [2, 1024], replicated
- pool_in_grad: float32 [3, 1024, 1024], P(None, None, 'mp')
- pool_out_grad: float32 [1024, 1024], P('mp')
- position_embed_grad: float32 [256, 1024], replicated
- lead_weight_grad: float32 [1024], replicated
- lead_bias_grad: float32 [1024], replicated
- first_gain_grad: float32 [1024], replicated
- first_shift_grad: float32 [1024], replicated
- attention_in_grad: float32 [3, 1024, 1024], P(None, None, 'mp')
- attention_out_grad: float32 [1024, 1024], P('mp')
- attention_bias_grad: float32 [1024], replicated
- second_gain_grad: float32 [1024], replicated
- second_shift_grad: float32 [1024], replicated
- up_weight_grad: float32 [1024, 4096], P(None, 'mp')
- up_bias_grad: float32 [4096], P('mp')
- down_weight_grad: float32 [4096, 1024], P('mp')
- down_bias_grad: float32 [1024], replicated
The draws below stay inside these ranges and needn't reach their ends.
Inputs may be any that keep to these rules, and one draw needn't show every extreme that they name: `variable_counts`: some item has all 48 slots live. `patch_counts`: some item has all 256 patches live.
All inputs are finite; a program needn't handle non-finite values.
Results may differ from the reference program's by a relative error of at most 0.0003.
Values sent between devices are 32-bit elements; how exact they have to be, the bound alone decides.
No kernel may reach another device: no remote copies, remote signals or barrier semaphores. Data moves between devices by JAX's collectives and lax.ppermute only.
A program may use at most 384 MiB of HBM per device.

```python
import math
import jax
import jax.numpy as jnp
from jax import lax

D = 1024
HEADS = 16
HD = 64
FF = 4096
NVAR = 48
PP = 4
NDATA = 2
TOK_DEV = 256
ITEMS = 8
TOKENS = 2048
N_DP = 8


def draw_variable_counts(key, part):
    key = jax.random.fold_in(key, 11)
    draw_key, pick_key = jax.random.split(key)
    counts = jax.random.randint(draw_key, (N_DP,), NVAR // 6, NVAR + 1)
    chosen = jax.random.randint(pick_key, (), 0, N_DP)
    return jnp.where(jnp.arange(N_DP) == chosen, NVAR, counts).astype(jnp.int32)


def draw_patch_counts(key, part):
    key = jax.random.fold_in(key, 23)
    draw_key, pick_key = jax.random.split(key)
    counts = jax.random.randint(draw_key, (N_DP,), TOK_DEV // 3, TOK_DEV + 1)
    chosen = jax.random.randint(pick_key, (), 0, N_DP)
    return jnp.where(jnp.arange(N_DP) == chosen, TOK_DEV, counts).astype(jnp.int32)


def set_ends(array, own_key, least, top_value):
    index_at = [jax.random.randint(jax.random.fold_in(own_key, axis), (), 0, length) for axis, length in enumerate(array.shape)]
    widest = array.shape.index(max(array.shape))
    next_to = index_at[:widest] + [(index_at[widest] + 1) % array.shape[widest]] + index_at[widest + 1:]
    return array.at[tuple(index_at)].set(least).at[tuple(next_to)].set(top_value)


def block_levels(own_key, dims, cuts, low, top_value):
    gain, own = 1.0, jax.random.fold_in(own_key, 6)
    for axis_at, shards_of in cuts:
        draws = jnp.exp(jax.random.uniform(jax.random.fold_in(own, axis_at), (shards_of,), jnp.float32, low / len(cuts), top_value / len(cuts)))
        gain = gain * jnp.repeat(draws, dims[axis_at] // shards_of).reshape([-1 if axis == axis_at else 1 for axis in range(len(dims))])
    return gain


def normal_values(own_key, dims, width, limit, pieces=(), kind=jnp.bfloat16):
    array = width * jax.random.normal(own_key, dims, jnp.float32)
    if pieces:
        array = array * block_levels(own_key, dims, pieces, -0.22, 0.18)
    return jnp.clip(array, -limit, limit).astype(kind)


def setup_inputs(seed: int = 0) -> dict:
    keys = jax.random.split(jax.random.key(seed), 28)
    return {
        "pixels": normal_values(keys[0], (TOKENS, NVAR * PP), 1.0, 6.0, ((0, 8),), jnp.float32),
        "variable_ids": jax.vmap(lambda own: jax.random.permutation(own, NVAR))(jax.random.split(keys[1], ITEMS)).reshape((ITEMS, NVAR)).astype(jnp.int32),
        "variable_counts": draw_variable_counts(jax.random.fold_in(keys[27], 71), 0),
        "lead_hours": set_ends(jax.random.randint(keys[3], (ITEMS,), 6, 169), jax.random.fold_in(keys[3], 1), 6, 168).astype(jnp.int32),
        "dataset_ids": set_ends(jax.random.randint(keys[4], (ITEMS,), 0, NDATA), jax.random.fold_in(keys[4], 1), 0, NDATA - 1).astype(jnp.int32),
        "patch_counts": draw_patch_counts(jax.random.fold_in(keys[27], 71), 0),
        "patch_weight": normal_values(keys[6], (NVAR, PP, D), PP ** -0.5, 3.0, (), jnp.float32),
        "patch_bias": normal_values(keys[7], (NVAR, D), 0.5, 3.0, (), jnp.float32),
        "variable_embed": normal_values(keys[8], (NVAR, D), 0.5, 3.0, (), jnp.float32),
        "pool_query": normal_values(keys[9], (NDATA, D), 1.0, 6.0, (), jnp.float32),
        "pool_in": normal_values(keys[10], (3, D, D), D ** -0.5, 0.1875, ((2, 4),), jnp.float32),
        "pool_out": normal_values(keys[11], (D, D), (max(D // 32, 1)) ** -0.5, 1.0, ((0, 4),), jnp.float32),
        "position_embed": normal_values(keys[12], (TOK_DEV, D), 0.5, 3.0, (), jnp.float32),
        "lead_weight": normal_values(keys[13], (D,), 1.0, 6.0, (), jnp.float32),
        "lead_bias": normal_values(keys[14], (D,), 0.5, 3.0, (), jnp.float32),
        "first_gain": jnp.clip(1.0 + 0.18 * jax.random.normal(keys[15], (D,), jnp.float32), 0.1, 1.9),
        "first_shift": normal_values(keys[16], (D,), 0.3, 1.75, (), jnp.float32),
        "attention_in": normal_values(keys[17], (3, D, D), D ** -0.5, 0.1875, ((2, 4),), jnp.float32),
        "attention_out": normal_values(keys[18], (D, D), (max(D // 128, 1)) ** -0.5, 2.0, ((0, 4),), jnp.float32),
        "attention_bias": normal_values(keys[19], (D,), 0.3, 1.75, (), jnp.float32),
        "second_gain": jnp.clip(1.0 + 0.18 * jax.random.normal(keys[20], (D,), jnp.float32), 0.1, 1.9),
        "second_shift": normal_values(keys[21], (D,), 0.3, 1.75, (), jnp.float32),
        "up_weight": normal_values(keys[22], (D, FF), D ** -0.5, 0.1875, ((1, 4),), jnp.float32),
        "up_bias": normal_values(keys[23], (FF,), 0.5, 3.0, ((0, 4),), jnp.float32),
        "down_weight": normal_values(keys[24], (FF, D), (FF // 4) ** -0.5, 0.1875, ((0, 4),), jnp.float32),
        "down_bias": normal_values(keys[25], (D,), 0.3, 1.75, (), jnp.float32),
        "cotangent": normal_values(keys[26], (TOKENS, D), 1.0, 6.0, ((0, 8),), jnp.float32),
    }


@jax.custom_vjp
def low(v):
    return lax.optimization_barrier(v.astype(jnp.bfloat16)).astype(jnp.float32)

@jax.custom_vjp
def low_back(v):
    return v

def low_keep(v):
    return (low(v), None)

def low_pass(kept, grad):
    return (grad,)

def back_keep(v):
    return (v, None)

def back_low(kept, grad):
    return (low(grad),)
low.defvjp(low_keep, low_pass)
low_back.defvjp(back_keep, back_low)
exact_mode = lax.Precision.HIGHEST

def layer_norm(values, norm_gain, norm_shift):
    centred = values - lax.optimization_barrier(jnp.mean(values, axis=-1, keepdims=True))
    spread = lax.optimization_barrier(jnp.mean(centred * centred, axis=-1, keepdims=True))
    return centred * lax.rsqrt(spread + 1e-06) * norm_gain + norm_shift

def item_forward(weight_set, pixel_rows, variable_row, variable_count, hours, dataset, patch_count):
    patch_weight, patch_bias, variable_embed, pool_query, pool_in, pool_out, position_embed, lead_weight, lead_bias, first_gain, first_shift, attention_in, attention_out, attention_bias, second_gain, second_shift, up_weight, up_bias, down_weight, down_bias = weight_set
    length = pixel_rows.shape[0]
    pixel_grid = pixel_rows.reshape(length, NVAR, PP)
    chosen = patch_weight[variable_row]
    offset = patch_bias[variable_row] + variable_embed[variable_row]
    embedded = jnp.einsum('tvp,vpd->tvd', pixel_grid, chosen, precision=exact_mode) + offset[None]
    query_heads = jnp.dot(pool_query[dataset], pool_in[0], precision=exact_mode).reshape(HEADS, HD)
    folded = jnp.einsum('dhe,he->dh', pool_in[1].reshape(D, HEADS, HD), query_heads, precision=exact_mode) / math.sqrt(HD)
    var_live = jnp.arange(NVAR) < variable_count
    scores = jnp.einsum('tvd,dh->tvh', embedded, folded, precision=exact_mode)
    scores = jnp.where(var_live[None, :, None], scores, -1e+30)
    weights_var = jax.nn.softmax(scores, axis=1)
    pooled = jnp.einsum('tvh,tvd->thd', weights_var, embedded, precision=exact_mode)
    mixed_heads = jnp.einsum('thd,dhe->the', pooled, pool_in[2].reshape(D, HEADS, HD), precision=exact_mode).reshape(length, D)
    lead_scale = hours.astype(jnp.float32) / 168.0
    block_input = jnp.dot(mixed_heads, pool_out, precision=exact_mode) + position_embed + lead_scale * lead_weight + lead_bias
    row_live = jnp.arange(length) < patch_count
    normed = layer_norm(block_input, first_gain, first_shift)
    projected = jnp.einsum('td,kde->kte', normed, attention_in, precision=exact_mode).reshape(3, length, HEADS, HD)
    token_scores = jnp.einsum('qhe,khe->hqk', projected[0], projected[1], precision=exact_mode) / math.sqrt(HD)
    token_scores = jnp.where(row_live[None, None, :], token_scores, -1e+30)
    attention_weights = jax.nn.softmax(token_scores, axis=-1)
    attended = jnp.einsum('hqk,khe->qhe', attention_weights, projected[2], precision=exact_mode).reshape(length, D)
    middle = block_input + jnp.dot(attended, attention_out, precision=exact_mode) + attention_bias
    normed_two = layer_norm(middle, second_gain, second_shift)
    hidden = jax.nn.gelu(jnp.dot(normed_two, up_weight, precision=exact_mode) + up_bias, approximate=False)
    result_rows = middle + jnp.dot(hidden, down_weight, precision=exact_mode) + down_bias
    return result_rows * row_live[:, None].astype(result_rows.dtype)

def reference(pixels, variable_ids, variable_counts, lead_hours, dataset_ids, patch_counts, patch_weight, patch_bias, variable_embed, pool_query, pool_in, pool_out, position_embed, lead_weight, lead_bias, first_gain, first_shift, attention_in, attention_out, attention_bias, second_gain, second_shift, up_weight, up_bias, down_weight, down_bias, cotangent):
    weight_set = (patch_weight, patch_bias, variable_embed, pool_query, pool_in, pool_out, position_embed, lead_weight, lead_bias, first_gain, first_shift, attention_in, attention_out, attention_bias, second_gain, second_shift, up_weight, up_bias, down_weight, down_bias)
    item_total = variable_ids.shape[0]
    pixel_items = pixels.reshape(item_total, TOK_DEV, NVAR * PP)

    def forward(weights_now, pixels_now):

        def one_item(carry, inputs):
            pixel_rows, variable_row, variable_count, hours, dataset, patch_count = inputs
            return (carry, item_forward(weights_now, pixel_rows, variable_row, variable_count, hours, dataset, patch_count))
        unused, outputs = lax.scan(jax.checkpoint(one_item), jnp.zeros((), jnp.float32), (pixels_now, variable_ids, variable_counts, lead_hours, dataset_ids, patch_counts))
        return outputs.reshape(item_total * TOK_DEV, D)
    block_output, pull_back = jax.vjp(forward, weight_set, pixel_items)
    weight_grads, pixel_grads = pull_back(cotangent)
    total = jnp.sum(patch_counts).astype(jnp.float32)
    scaled = [grad_part / total for grad_part in weight_grads]
    return (block_output, pixel_grads.reshape(item_total * TOK_DEV, NVAR * PP), scaled[0], scaled[1], scaled[2], scaled[3], scaled[4], scaled[5], scaled[6], scaled[7], scaled[8], scaled[9], scaled[10], scaled[11], scaled[12], scaled[13], scaled[14], scaled[15], scaled[16], scaled[17], scaled[18], scaled[19])
```

```python
import functools
import math

import jax
import jax.numpy as jnp
from jax import lax
from jax.experimental import pallas as pl
from jax.experimental.pallas import tpu as pltpu
from jax.sharding import PartitionSpec as P

HD = 64
NVAR = 48
PP = 4
NDATA = 2
GROUPS = 8
SPLITS = 4

exact = lax.Precision.HIGH


def dot(left, right, contract):
    return lax.dot_general(left, right, (contract, ((), ())), precision=exact, preferred_element_type=jnp.float32)


def mm(left, right):
    return dot(left, right, ((1,), (0,)))


def mm_t(left, right):
    return dot(left, right, ((1,), (1,)))


def t_mm(left, right):
    return dot(left, right, ((0,), (0,)))


def together(*values):
    return lax.optimization_barrier(values)


def rows_of(array, place, count):
    return lax.dynamic_slice_in_dim(array, place * count, count)


def is_direct():
    return lax.axis_size("dp") == GROUPS and lax.axis_size("mp") == SPLITS


def dp_swap(array, away):
    return lax.ppermute(array, "dp", [(i, i ^ away) for i in range(GROUPS)])


def mp_swap(array, away):
    return lax.ppermute(array, "mp", [(i, i ^ away) for i in range(SPLITS)])


def lay_kernel(starts_ref, *refs):
    pieces, merged, sems = refs[:-2], refs[-2], refs[-1]
    copies = []
    for k, piece in enumerate(pieces):
        rows = piece.shape[0]
        target = merged.at[pl.ds(pl.multiple_of(starts_ref[k], rows), rows), :]
        copies.append(pltpu.make_async_copy(piece, target, sems.at[k]))
    for copy in copies:
        copy.start()
    for copy in copies:
        copy.wait()


def lay_together(starts, pieces, total_rows):
    shape = (total_rows,) + pieces[0].shape[1:]
    return pl.pallas_call(
        lay_kernel,
        out_shape=jax.ShapeDtypeStruct(shape, pieces[0].dtype),
        in_specs=[pl.BlockSpec(memory_space=pltpu.SMEM)] + [pl.BlockSpec(memory_space=pl.ANY)] * len(pieces),
        out_specs=pl.BlockSpec(memory_space=pltpu.VMEM),
        scratch_shapes=[pltpu.SemaphoreType.DMA((len(pieces),))],
        compiler_params=pltpu.CompilerParams(vmem_limit_bytes=16 * 1024 * 1024),
        cost_estimate=pl.CostEstimate(flops=0, bytes_accessed=2 * math.prod(shape) * 4, transcendentals=0),
        name="lay_together",
    )(jnp.stack(starts).astype(jnp.int32), *pieces)


class Round:
    def __init__(self, rows):
        self.direct, self.count = is_direct(), rows.shape[0]
        if not self.direct:
            return
        order = [i for i in range(0, GROUPS, 2)] + [i for i in reversed(range(1, GROUPS, 2))]
        self.right = [(order[i], order[(i + 1) % GROUPS]) for i in range(GROUPS)]
        self.left = [(b, a) for a, b in self.right]
        own = lax.axis_index("dp")
        self.place = jnp.where(own % 2 == 0, own // 2, GROUPS - 1 - own // 2)
        self.step, self.held = 0, (rows, rows)
        self.pieces, self.starts = [rows], [self.place * self.count]

    def send(self):
        if not self.direct:
            return ()
        self.step += 1
        one, two = self.held
        if self.step == GROUPS // 2:
            one, two = one[: self.count // 2], two[self.count // 2 :]
        return lax.ppermute(one, "dp", self.right), lax.ppermute(two, "dp", self.left)

    def land(self, came):
        if not self.direct:
            return
        self.held = came
        skip = self.count // 2 if self.step == GROUPS // 2 else 0
        self.pieces += list(came)
        for away, more in ((-self.step, 0), (self.step, skip)):
            self.starts.append(lax.rem(self.place + (away + GROUPS), GROUPS) * self.count + more)

    def merged(self):
        return lay_together(self.starts, self.pieces, GROUPS * self.count)


def side():
    return lax.axis_index("mp") % 2


class MpSum:
    def __init__(self, array):
        self.held, self.direct = array, is_direct()

    def start(self):
        if not self.direct:
            return lax.psum(self.held, "mp")
        return mp_swap(rows_of(self.held, 1 - side(), self.held.shape[0] // 2), 1)

    def cross(self, came):
        if not self.direct:
            self.held = came
            return ()
        self.held = rows_of(self.held, side(), self.held.shape[0] // 2) + came
        return mp_swap(self.held, 2)

    def finish(self, came):
        if not self.direct:
            return self.held
        mine = self.held + came
        other = mp_swap(mine, 1)
        first = side() == 0
        return jnp.concatenate([jnp.where(first, mine, other), jnp.where(first, other, mine)], axis=0)


def mp_gather(array):
    if not is_direct():
        return lax.all_gather(array, "mp", axis=0, tiled=True)
    own = lax.axis_index("mp")
    rows = array.shape[0]
    far = mp_swap(array, 2)
    near = mp_swap(jnp.concatenate([array, far], axis=0), 1)
    pieces = [array, far, near[:rows], near[rows:]]
    return lay_together([(own ^ k) * rows for k in (0, 2, 1, 3)], pieces, SPLITS * rows)


def normalise(values):
    centred = values - jnp.mean(values, axis=-1, keepdims=True)
    inverse = lax.rsqrt(jnp.mean(centred * centred, axis=-1, keepdims=True) + 1e-06)
    return centred * inverse, inverse


def activate(values):
    phi_sum = 0.5 * (1.0 + lax.erf(values * math.sqrt(0.5)))
    phi = jnp.exp(-0.5 * values * values) * (1.0 / math.sqrt(2.0 * math.pi))
    return values * phi_sum, phi_sum + values * phi


def normalise_back(grad, hat, inverse):
    return (grad - jnp.mean(grad, axis=-1, keepdims=True) - hat * jnp.mean(grad * hat, axis=-1, keepdims=True)) * inverse


def full(left, right, contract=((1,), (0,))):
    return lax.dot_general(
        left, right, (contract, ((), ())), precision=lax.Precision.HIGHEST, preferred_element_type=jnp.float32
    )


def across_lanes(shape):
    return lax.broadcasted_iota(jnp.int32, shape, len(shape) - 1)


def down_rows(shape):
    return lax.broadcasted_iota(jnp.int32, shape, 0)


def chosen(condition):
    return jnp.where(condition, 1.0, 0.0).astype(jnp.float32)


PIXEL_ROWS = NVAR * PP


def holds(rows, columns, head):
    place, column = down_rows((rows, columns)), across_lanes((rows, columns))
    return chosen(column == head * NVAR + place // PP)


def same_head(columns):
    return chosen(down_rows((columns, columns)) // NVAR == across_lanes((columns, columns)) // NVAR)


def mover_of(ids_row):
    shape = (PIXEL_ROWS, NVAR)
    slot_ids = jnp.where(down_rows(shape) // PP == across_lanes(shape), ids_row, 0)
    wanted = jnp.sum(slot_ids, axis=1, keepdims=True)
    shape = (PIXEL_ROWS, PIXEL_ROWS)
    return chosen(wanted * PP + down_rows(shape) % PP == across_lanes(shape))


def pool_kernel(
    heads, facts_ref, ids_ref, pixels_ref, weight_ref, bias_ref, embed_ref, query_ref, in_ref, out_ref,
    part_ref, places_ref, w_ref, pooled_ref, keys_ref, values_ref, queries_ref, table_ref, folded_ref,
):
    columns, width = heads * NVAR, heads * HD
    dataset, live_count = facts_ref[0], facts_ref[1]
    ids_row = ids_ref[...]
    places = full(pixels_ref[...], mover_of(ids_row))
    places_ref[...] = places
    table_ref[:PIXEL_ROWS] = weight_ref[...]
    table_ref[PIXEL_ROWS:] = bias_ref[...] + embed_ref[...]
    table = table_ref[...]
    keys_ref[...] = full(table, in_ref[1])
    values_ref[...] = full(table, in_ref[2])
    queries = full(query_ref[...], in_ref[0])
    queries_ref[...] = queries
    query = jnp.sum(jnp.where(down_rows(queries.shape) == dataset, queries, 0.0), axis=0, keepdims=True)
    query = query * (1.0 / math.sqrt(HD))
    of_head = chosen(down_rows((width, columns)) // HD == across_lanes((width, columns)) // NVAR)
    keys = keys_ref[...] * query
    wide = full(keys, of_head)
    pixel_shape, offset_shape = (PIXEL_ROWS, columns), (NVAR, columns)
    pixel_scores = jnp.where(down_rows(pixel_shape) // PP == across_lanes(pixel_shape) % NVAR, wide[:PIXEL_ROWS], 0.0)
    offset_scores = jnp.where(down_rows(offset_shape) == across_lanes(offset_shape) % NVAR, wide[PIXEL_ROWS:], 0.0)
    scores = full(places, pixel_scores) + jnp.sum(offset_scores, axis=0, keepdims=True)
    square = (NVAR, NVAR)
    ids_down = jnp.sum(jnp.where(down_rows(square) == across_lanes(square), ids_row, 0), axis=1, keepdims=True)
    alive = (ids_down == across_lanes(offset_shape) % NVAR) & (down_rows(offset_shape) < live_count)
    live = jnp.sum(chosen(alive), axis=0, keepdims=True)
    scores = jnp.where(live > 0.5, scores, -1e30)
    head_at = across_lanes(scores.shape) // NVAR
    largest = jnp.zeros_like(scores)
    for h in range(heads):
        top = jnp.max(jnp.where(head_at == h, scores, -1e30), axis=1, keepdims=True)
        largest = jnp.where(head_at == h, top, largest)
    powers = jnp.exp(scores - largest)
    weights = powers / full(powers, same_head(columns))
    w_ref[...] = weights
    values = values_ref[...]
    offsets = full(holds_variable(heads), values[PIXEL_ROWS:])
    offsets = jnp.where(down_rows(offsets.shape) // NVAR == across_lanes(offsets.shape) // HD, offsets, 0.0)
    pooled = full(weights, offsets)
    for h in range(heads):
        mixed = full(weights, holds(PIXEL_ROWS, columns, h), ((1,), (1,))) * places
        part = full(mixed, values[:PIXEL_ROWS])
        pooled = pooled + jnp.where(across_lanes(part.shape) // HD == h, part, 0.0)
    pooled_ref[...] = pooled
    part_ref[...] = full(pooled, out_ref[...])
    rows = (8, width)
    by_head = jnp.where(across_lanes(rows) // HD == down_rows(rows), query, 0.0)
    folded_ref[...] = full(by_head, keys_ref[:PIXEL_ROWS], ((1,), (1,)))


def holds_variable(heads):
    shape = (heads * NVAR, NVAR)
    return chosen(down_rows(shape) % NVAR == across_lanes(shape))


def pool_back_kernel(
    heads, ids_ref, grad_ref, out_ref, places_ref, w_ref, values_ref, folded_ref,
    pixel_ref, value_raw_ref, score_raw_ref, offset_raw_ref,
):
    columns = heads * NVAR
    weights, places, values = w_ref[...], places_ref[...], values_ref[...]
    g_pool = full(grad_ref[...], out_ref[...], ((1,), (1,)))
    variable = holds_variable(heads)
    offsets = full(variable, values[PIXEL_ROWS:])
    own_head = down_rows(offsets.shape) // NVAR == across_lanes(offsets.shape) // HD
    g_pw = full(g_pool, jnp.where(own_head, offsets, 0.0), ((1,), (1,)))
    backs, mixes, g_heads = [], [], []
    for h in range(heads):
        g_head = jnp.where(across_lanes(g_pool.shape) // HD == h, g_pool, 0.0)
        back = full(g_head, values[:PIXEL_ROWS], ((1,), (1,)))
        holder = holds(PIXEL_ROWS, columns, h)
        g_pw = g_pw + full(places * back, holder)
        backs.append(back)
        g_heads.append(g_head)
    weighted = weights * g_pw
    g_ps = weighted - weights * full(weighted, same_head(columns))
    g_places = jnp.zeros_like(places)
    value_raw = jnp.zeros_like(values[:PIXEL_ROWS])
    score_raw_ref[...] = jnp.zeros_like(score_raw_ref)
    for h in range(heads):
        holder = holds(PIXEL_ROWS, columns, h)
        w_wide = full(weights, holder, ((1,), (1,)))
        g_wide = full(g_ps, holder, ((1,), (1,)))
        score_raw_ref[h : h + 1] = jnp.sum(places * g_wide, axis=0, keepdims=True)
        value_raw = value_raw + full(w_wide * places, g_heads[h], ((0,), (0,)))
        g_places = g_places + g_wide * folded_ref[h : h + 1] + w_wide * backs[h]
    value_raw_ref[:PIXEL_ROWS] = value_raw
    offset_values = jnp.where(own_head, full(weights, g_pool, ((0,), (0,))), 0.0)
    value_raw_ref[PIXEL_ROWS:] = full(variable, offset_values, ((0,), (0,)))
    rows = (8, columns)
    by_head = jnp.where(across_lanes(rows) // NVAR == down_rows(rows), jnp.sum(g_ps, axis=0, keepdims=True), 0.0)
    offset_raw_ref[...] = full(by_head, variable)
    pixel_ref[...] = full(g_places, mover_of(ids_ref[...]), ((1,), (1,)))


def in_vmem(kernel, name, outs, scalars, arrays, flops, limit):
    held = pl.BlockSpec(memory_space=pltpu.VMEM)
    return pl.pallas_call(
        kernel,
        out_shape=[jax.ShapeDtypeStruct(shape, jnp.float32) for shape in outs],
        in_specs=[pl.BlockSpec(memory_space=pltpu.SMEM)] * len(scalars) + [held] * len(arrays),
        out_specs=[held] * len(outs),
        compiler_params=pltpu.CompilerParams(vmem_limit_bytes=limit * 1024 * 1024),
        cost_estimate=pl.CostEstimate(flops=flops, bytes_accessed=sum(a.size for a in arrays) * 4, transcendentals=0),
        name=name,
    )(*scalars, *arrays)


def cut_kernel(block_ref, in_ref, out_ref, pool_ref):
    step = pl.program_id(0)
    block = block_ref[...]

    @pl.when(step < 3)
    def _():
        in_ref[...] = block

    @pl.when(step == 3)
    def _():
        out_ref[...] = block.T

    @pl.when(step == 4)
    def _():
        pool_ref[...] = block.T


def cut_apart(stacked):
    width, local = stacked.shape[0] // 5, stacked.shape[1]
    return pl.pallas_call(
        cut_kernel,
        grid=(5,),
        out_shape=[
            jax.ShapeDtypeStruct((3 * width, local), jnp.float32),
            jax.ShapeDtypeStruct((local, width), jnp.float32),
            jax.ShapeDtypeStruct((local, width), jnp.float32),
        ],
        in_specs=[pl.BlockSpec((width, local), lambda i: (i, 0))],
        out_specs=[
            pl.BlockSpec((width, local), lambda i: (jnp.minimum(i, 2), 0)),
            pl.BlockSpec((local, width), lambda i: (0, 0)),
            pl.BlockSpec((local, width), lambda i: (0, 0)),
        ],
        compiler_params=pltpu.CompilerParams(vmem_limit_bytes=24 * 1024 * 1024),
        cost_estimate=pl.CostEstimate(flops=0, bytes_accessed=8 * stacked.size, transcendentals=0),
        name="cut_apart",
    )(stacked)


def shards(
    pixels,
    variable_ids,
    variable_counts,
    lead_hours,
    dataset_ids,
    patch_counts,
    patch_weight,
    patch_bias,
    variable_embed,
    pool_query,
    pool_in,
    pool_out,
    position_embed,
    lead_weight,
    lead_bias,
    first_gain,
    first_shift,
    attention_in,
    attention_out,
    attention_bias,
    second_gain,
    second_shift,
    up_weight,
    up_bias,
    down_weight,
    down_bias,
    cotangent,
):
    direct = is_direct()
    length, width = cotangent.shape
    heads = pool_out.shape[0] // HD
    table_rows = NVAR * (PP + 1)
    key_live = jnp.arange(length) < patch_counts[0]
    row_mask = key_live.astype(jnp.float32)[:, None]
    lead_scale = lead_hours[0].astype(jnp.float32) / 168.0
    pick_set = (dataset_ids[0] == jnp.arange(NDATA)).astype(jnp.float32)
    grad_rows = cotangent * row_mask
    half_rows = length // 2
    grads_round = Round(rows_of(grad_rows, side(), half_rows))
    grads_came = grads_round.send()
    count = jnp.full((8, 128), patch_counts[0].astype(jnp.float32))

    def count_send(away):
        return dp_swap(count, away) if direct else 0.0

    if not direct:
        count = lax.psum(count, "dp")
    count_came = count_send(1)

    local = heads * HD
    columns = heads * NVAR
    facts = jnp.concatenate([dataset_ids, variable_counts]).astype(jnp.int32)
    query_rows = jnp.pad(pool_query, ((0, 8 - NDATA), (0, 0)))
    pool_part, places, pool_w, pooled, key_table, value_table, queries, table, folded = in_vmem(
        functools.partial(pool_kernel, heads),
        "pool",
        [
            (length, width), (length, PIXEL_ROWS), (length, columns), (length, local), (table_rows, local),
            (table_rows, local), (8, local), (table_rows, width), (8, PIXEL_ROWS),
        ],
        [facts],
        [
            variable_ids, pixels, patch_weight.reshape(PIXEL_ROWS, width), patch_bias, variable_embed, query_rows,
            pool_in, pool_out,
        ],
        10**9,
        40,
    )
    pool_sum = MpSum(pool_part)
    across = pool_sum.cross(pool_sum.start())
    across, grads_came, count_came = together(across, grads_came, count_came)
    count = count + count_came
    count_came = count_send(2)
    block_input = pool_sum.finish(across) + position_embed + lead_scale * lead_weight + lead_bias
    grads_round.land(grads_came)
    grads_came = grads_round.send()

    hat_one, inverse_one = normalise(block_input)
    norm_one = hat_one * first_gain + first_shift
    att_q, att_k, att_v = [mm(norm_one, attention_in[j]) for j in range(3)]

    def in_heads(array):
        return [array[:, h * HD : (h + 1) * HD] for h in range(heads)]

    q_heads, k_heads, v_heads = in_heads(att_q), in_heads(att_k), in_heads(att_v)
    att_w = []
    for h in range(heads):
        token_scores = mm_t(q_heads[h], k_heads[h]) / math.sqrt(HD)
        att_w.append(jax.nn.softmax(jnp.where(key_live[None, :], token_scores, -1e30), axis=1))
    attended = jnp.concatenate([mm(att_w[h], v_heads[h]) for h in range(heads)], axis=1)
    attention_sum = MpSum(mm(attended, attention_out))
    near, grads_came = together(attention_sum.start(), grads_came)
    across = attention_sum.cross(near)
    grads_round.land(grads_came)
    grads_came = grads_round.send()
    g_hidden = mm_t(grad_rows, down_weight)
    across, grads_came, count_came, g_hidden = together(across, grads_came, count_came, g_hidden)
    count = count + count_came
    count_came = count_send(4)
    middle = block_input + attention_sum.finish(across) + attention_bias
    grads_round.land(grads_came)
    grads_came = grads_round.send()

    hat_two, inverse_two = normalise(middle)
    norm_two = hat_two * second_gain + second_shift
    norm_round = Round(rows_of(norm_two, side(), half_rows))
    norm_came = norm_round.send()
    up_pre, grads_came = together(mm(norm_two, up_weight) + up_bias, grads_came)
    grads_round.land(grads_came)
    hidden, slope = activate(up_pre)
    g_up = g_hidden * slope
    back_sum = MpSum(mm_t(g_up, up_weight))
    near, norm_came = together(back_sum.start(), norm_came)
    across = back_sum.cross(near)
    norm_round.land(norm_came)
    norm_came = norm_round.send()
    back_mine = grads_other = ()
    if direct:
        grads_mine = grads_round.merged()
        grads_other = mp_swap(grads_mine, 1)
        back_mine = mm_t(grads_mine, down_weight)
    across, norm_came, back_mine, count_came = together(across, norm_came, back_mine, count_came)
    scale = 1.0 / (count + count_came)[0, 0]
    g_n2 = back_sum.finish(across)
    norm_round.land(norm_came)
    norm_came = norm_round.send()
    g_middle = grad_rows + normalise_back(g_n2 * second_gain, hat_two, inverse_two)
    output_sum = MpSum(mm(hidden, down_weight))
    output_across = output_sum.cross(output_sum.start())

    g_att = in_heads(mm_t(g_middle, attention_out))
    g_q, g_k, g_v = [], [], []
    for h in range(heads):
        g_w = mm_t(g_att[h], v_heads[h])
        g_s = att_w[h] * (g_w - jnp.sum(att_w[h] * g_w, axis=1, keepdims=True)) / math.sqrt(HD)
        g_q.append(mm(g_s, k_heads[h]))
        g_k.append(t_mm(g_s, q_heads[h]))
        g_v.append(t_mm(att_w[h], g_att[h]))
    g_qkv = [jnp.concatenate(g, axis=1) for g in (g_q, g_k, g_v)]
    g_n1_part = mm_t(g_qkv[0], attention_in[0]) + mm_t(g_qkv[1], attention_in[1]) + mm_t(g_qkv[2], attention_in[2])
    input_sum = MpSum(g_n1_part)
    near, norm_came, output_across, g_later, attended = together(
        input_sum.start(), norm_came, output_across, g_qkv, attended
    )
    across = input_sum.cross(near)
    norm_round.land(norm_came)
    norm_came = norm_round.send()
    raw = [t_mm(norm_one, g * scale) for g in g_later] + [t_mm(g_middle, attended * scale)]
    raw = jnp.concatenate(raw + [jnp.zeros((width, heads * HD), jnp.float32)], axis=0)
    across, norm_came, raw = together(across, norm_came, raw)
    g_n1 = input_sum.finish(across)
    norm_round.land(norm_came)
    g_input = g_middle + normalise_back(g_n1 * first_gain, hat_one, inverse_one)

    pool_out_raw, g_input = together(t_mm(g_input, pooled * scale), g_input)
    raw = lax.dynamic_update_slice_in_dim(raw, pool_out_raw, 4 * width, 0)
    norm_pieces = norm_round.pieces if direct else ()
    raw, norm_pieces, grads_later = together(raw, norm_pieces, grads_other)
    raw_part = lax.psum_scatter(raw, "dp", scatter_dimension=0, tiled=True)
    pixel_part, value_raw, score_raw, offset_raw = in_vmem(
        functools.partial(pool_back_kernel, heads),
        "pool_back",
        [(length, PIXEL_ROWS), (table_rows, local), (8, PIXEL_ROWS), (8, NVAR)],
        [],
        [variable_ids, g_input, pool_out, places, pool_w, value_table, folded],
        10**9,
        40,
    )
    score_raw = jnp.concatenate([score_raw, offset_raw], axis=1)[:heads]
    score_raw = (pick_set[:, None, None] * score_raw[None]).reshape(NDATA * heads, table_rows)
    score_raw = jnp.pad(score_raw, ((0, 0), (0, local - table_rows)))
    lead_bias_raw = jnp.sum(g_input, axis=0)
    vectors = jnp.stack([
        lead_scale * lead_bias_raw,
        lead_bias_raw,
        jnp.sum(g_n1 * hat_one, axis=0),
        jnp.sum(g_n1, axis=0),
        jnp.sum(g_middle, axis=0),
        jnp.sum(g_n2 * hat_two, axis=0),
        jnp.sum(g_n2, axis=0),
        jnp.sum(g_up, axis=0),
        jnp.sum(grad_rows, axis=0),
    ])
    own = lax.axis_index("mp")
    quarter = length // lax.axis_size("mp")
    small = [value_raw, score_raw, vectors.reshape(-1, local)]
    used = sum(piece.shape[0] for piece in small)
    filler = jnp.zeros((-used % 8, local), jnp.float32)
    small = jnp.concatenate(small + [filler, rows_of(g_input, own, quarter).reshape(-1, local)], axis=0)

    def small_send(away):
        return dp_swap(small, away) if direct else 0.0

    if not direct:
        small = lax.psum(small, "dp")
    up_mine = up_other = down_sum = slope = up_sum = back_other = ()
    if direct:
        norm_round.pieces = norm_pieces
        norm_mine = norm_round.merged()
        norm_other = mp_swap(norm_mine, 1)
        up_mine = mm(norm_mine, up_weight)
        back_other = mm_t(grads_later, down_weight)
    small_came, up_mine, back_other, output_across = together(small_send(1), up_mine, back_other, output_across)
    block_output = (middle + output_sum.finish(output_across) + down_bias) * row_mask
    small = small + small_came
    if direct:
        hidden, slope = activate(up_mine + up_bias)
        down_sum = t_mm(hidden * scale, grads_mine)
    small_came, down_sum, slope = together(small_send(2), down_sum, slope)
    small = small + small_came
    small_came = small_send(4)
    if direct:
        up_sum = t_mm(norm_mine, back_mine * slope * scale)
        up_other = mm(norm_other, up_weight)
    small_came, up_sum, up_other, raw_part = together(small_came, up_sum, up_other, raw_part)
    raw_sum = lax.all_gather(raw_part, "dp", axis=0, tiled=True)
    small = (small + small_came) * scale
    value_sum = small[:table_rows]
    score_sum = small[table_rows : table_rows + NDATA * heads, :table_rows]
    vector_sums = small[table_rows + NDATA * heads : used].reshape(-1, width)
    position_sum = mp_gather(small[used + -used % 8 :].reshape(quarter, width))

    by_head = jnp.arange(local)[None, :] // HD == jnp.arange(NDATA * heads)[:, None] % heads
    by_head = by_head.astype(jnp.float32) / math.sqrt(HD)
    key_sum = t_mm(score_sum, by_head * jnp.repeat(queries[:NDATA], heads, axis=0))
    query_grad = jnp.sum((mm(score_sum, key_table) * by_head).reshape(NDATA, heads, local), axis=1)
    table_part = mm_t(key_sum, pool_in[1]) + mm_t(value_sum, pool_in[2])
    pool_query_part = mm_t(query_grad, pool_in[0])
    rest = length - (table_rows + NDATA)
    table_part = jnp.concatenate([table_part, pool_query_part, jnp.zeros((rest, width), jnp.float32)], axis=0)
    wide = jnp.concatenate([table_part, pixel_part], axis=1)
    table_sum = MpSum(wide)
    across = table_sum.cross(table_sum.start())
    if direct:
        hidden, slope = activate(up_other + up_bias)
        down_sum = down_sum + t_mm(hidden * scale, grads_other)
    across, down_sum, slope = together(across, down_sum, slope)
    sums = table_sum.finish(across)
    table_sums, pixels_grad = sums[:, :width], sums[:, width:]
    patch_weight_grad = table_sums[: NVAR * PP].reshape(NVAR, PP, width)
    offset_grad = table_sums[NVAR * PP : table_rows]
    pool_query_grad = table_sums[table_rows : table_rows + NDATA]
    lower = jnp.zeros((NDATA, value_sum.shape[1]), jnp.float32)
    upper = jnp.zeros((table_rows, value_sum.shape[1]), jnp.float32)
    pool_in_grad = lax.dot_general(
        jnp.stack([jnp.concatenate(pair, axis=0) for pair in ((upper, query_grad), (key_sum, lower), (value_sum, lower))]),
        jnp.concatenate([table, pool_query], axis=0),
        (((1,), (0,)), ((), ())),
        precision=exact,
    ).transpose(0, 2, 1)

    if direct:
        up_sum = up_sum + t_mm(norm_other, back_other * slope * scale)
    else:
        down_sum = lax.psum(t_mm(hidden, grad_rows), "dp") * scale
        up_sum = lax.psum(t_mm(norm_two, g_up), "dp") * scale
    raw_sum, up_sum = together(raw_sum, up_sum)
    attention_in_sum, attention_out_sum, pool_out_sum = cut_apart(raw_sum)
    return (
        block_output,
        pixels_grad,
        patch_weight_grad,
        offset_grad,
        offset_grad,
        pool_query_grad,
        pool_in_grad,
        pool_out_sum,
        position_sum,
        vector_sums[0],
        vector_sums[1],
        vector_sums[2],
        vector_sums[3],
        attention_in_sum.reshape(attention_in.shape),
        attention_out_sum,
        vector_sums[4],
        vector_sums[5],
        vector_sums[6],
        up_sum,
        vector_sums[7],
        down_sum,
        vector_sums[8],
    )


def solution(mesh):
    return jax.shard_map(
        shards,
        mesh=mesh,
        in_specs=(
            P("dp", None),
            P("dp", None),
            P("dp"),
            P("dp"),
            P("dp"),
            P("dp"),
            P(),
            P(),
            P(),
            P(),
            P(None, None, "mp"),
            P("mp", None),
            P(),
            P(),
            P(),
            P(),
            P(),
            P(None, None, "mp"),
            P("mp", None),
            P(),
            P(),
            P(),
            P(None, "mp"),
            P("mp"),
            P("mp", None),
            P(),
            P("dp", None),
        ),
        out_specs=(
            P("dp", None),
            P("dp", None),
            P(),
            P(),
            P(),
            P(),
            P(None, None, "mp"),
            P("mp", None),
            P(),
            P(),
            P(),
            P(),
            P(),
            P(None, None, "mp"),
            P("mp", None),
            P(),
            P(),
            P(),
            P(None, "mp"),
            P("mp"),
            P("mp", None),
            P(),
        ),
        check_vma=False,
    )
```

```python
import functools
import math

import jax
import jax.numpy as jnp
from jax import lax
from jax.experimental import pallas as pl
from jax.experimental.pallas import tpu as pltpu
from jax.sharding import PartitionSpec as P

HD = 64
NVAR = 48
PP = 4
NDATA = 2
GROUPS = 8
SPLITS = 4

exact = lax.Precision.HIGH


def dot(left, right, contract):
    return lax.dot_general(left, right, (contract, ((), ())), precision=exact, preferred_element_type=jnp.float32)


def mm(left, right):
    return dot(left, right, ((1,), (0,)))


def mm_t(left, right):
    return dot(left, right, ((1,), (1,)))


def t_mm(left, right):
    return dot(left, right, ((0,), (0,)))


def together(*values):
    return lax.optimization_barrier(values)


def rows_of(array, place, count):
    return lax.dynamic_slice_in_dim(array, place * count, count)


def is_direct():
    return lax.axis_size("dp") == GROUPS and lax.axis_size("mp") == SPLITS


def dp_swap(array, away):
    return lax.ppermute(array, "dp", [(i, i ^ away) for i in range(GROUPS)])


def mp_swap(array, away):
    return lax.ppermute(array, "mp", [(i, i ^ away) for i in range(SPLITS)])


def lay_kernel(starts_ref, *refs):
    pieces, merged, sems = refs[:-2], refs[-2], refs[-1]
    copies = []
    for k, piece in enumerate(pieces):
        rows = piece.shape[0]
        target = merged.at[pl.ds(pl.multiple_of(starts_ref[k], rows), rows), :]
        copies.append(pltpu.make_async_copy(piece, target, sems.at[k]))
    for copy in copies:
        copy.start()
    for copy in copies:
        copy.wait()


def lay_together(starts, pieces, total_rows):
    shape = (total_rows,) + pieces[0].shape[1:]
    return pl.pallas_call(
        lay_kernel,
        out_shape=jax.ShapeDtypeStruct(shape, pieces[0].dtype),
        in_specs=[pl.BlockSpec(memory_space=pltpu.SMEM)] + [pl.BlockSpec(memory_space=pl.ANY)] * len(pieces),
        out_specs=pl.BlockSpec(memory_space=pltpu.VMEM),
        scratch_shapes=[pltpu.SemaphoreType.DMA((len(pieces),))],
        compiler_params=pltpu.CompilerParams(vmem_limit_bytes=16 * 1024 * 1024),
        cost_estimate=pl.CostEstimate(flops=0, bytes_accessed=2 * math.prod(shape) * 4, transcendentals=0),
        name="lay_together",
    )(jnp.stack(starts).astype(jnp.int32), *pieces)


class Round:
    def __init__(self, rows):
        self.direct, self.count = is_direct(), rows.shape[0]
        if not self.direct:
            return
        order = [i for i in range(0, GROUPS, 2)] + [i for i in reversed(range(1, GROUPS, 2))]
        self.right = [(order[i], order[(i + 1) % GROUPS]) for i in range(GROUPS)]
        self.left = [(b, a) for a, b in self.right]
        own = lax.axis_index("dp")
        self.place = jnp.where(own % 2 == 0, own // 2, GROUPS - 1 - own // 2)
        self.step, self.held = 0, (rows, rows)
        self.pieces, self.starts = [rows], [self.place * self.count]

    def send(self):
        if not self.direct:
            return ()
        self.step += 1
        one, two = self.held
        if self.step == GROUPS // 2:
            one, two = one[: self.count // 2], two[self.count // 2 :]
        return lax.ppermute(one, "dp", self.right), lax.ppermute(two, "dp", self.left)

    def land(self, came):
        if not self.direct:
            return
        self.held = came
        skip = self.count // 2 if self.step == GROUPS // 2 else 0
        self.pieces += list(came)
        for away, more in ((-self.step, 0), (self.step, skip)):
            self.starts.append(lax.rem(self.place + (away + GROUPS), GROUPS) * self.count + more)

    def merged(self):
        return lay_together(self.starts, self.pieces, GROUPS * self.count)


def side():
    return lax.axis_index("mp") % 2


class MpSum:
    def __init__(self, array):
        self.held, self.direct = array, is_direct()

    def start(self):
        if not self.direct:
            return lax.psum(self.held, "mp")
        return mp_swap(rows_of(self.held, 1 - side(), self.held.shape[0] // 2), 1)

    def cross(self, came):
        if not self.direct:
            self.held = came
            return ()
        self.held = rows_of(self.held, side(), self.held.shape[0] // 2) + came
        return mp_swap(self.held, 2)

    def finish(self, came):
        if not self.direct:
            return self.held
        mine = self.held + came
        other = mp_swap(mine, 1)
        first = side() == 0
        return jnp.concatenate([jnp.where(first, mine, other), jnp.where(first, other, mine)], axis=0)


def mp_gather(array):
    if not is_direct():
        return lax.all_gather(array, "mp", axis=0, tiled=True)
    own = lax.axis_index("mp")
    rows = array.shape[0]
    far = mp_swap(array, 2)
    near = mp_swap(jnp.concatenate([array, far], axis=0), 1)
    pieces = [array, far, near[:rows], near[rows:]]
    return lay_together([(own ^ k) * rows for k in (0, 2, 1, 3)], pieces, SPLITS * rows)


def normalise(values):
    centred = values - jnp.mean(values, axis=-1, keepdims=True)
    inverse = lax.rsqrt(jnp.mean(centred * centred, axis=-1, keepdims=True) + 1e-06)
    return centred * inverse, inverse


def activate(values):
    phi_sum = 0.5 * (1.0 + lax.erf(values * math.sqrt(0.5)))
    phi = jnp.exp(-0.5 * values * values) * (1.0 / math.sqrt(2.0 * math.pi))
    return values * phi_sum, phi_sum + values * phi


def normalise_back(grad, hat, inverse):
    return (grad - jnp.mean(grad, axis=-1, keepdims=True) - hat * jnp.mean(grad * hat, axis=-1, keepdims=True)) * inverse


def full(left, right, contract=((1,), (0,))):
    return lax.dot_general(
        left, right, (contract, ((), ())), precision=lax.Precision.HIGHEST, preferred_element_type=jnp.float32
    )


def across_lanes(shape):
    return lax.broadcasted_iota(jnp.int32, shape, len(shape) - 1)


def down_rows(shape):
    return lax.broadcasted_iota(jnp.int32, shape, 0)


def chosen(condition):
    return jnp.where(condition, 1.0, 0.0).astype(jnp.float32)


PIXEL_ROWS = NVAR * PP


def holds(rows, columns, head):
    place, column = down_rows((rows, columns)), across_lanes((rows, columns))
    return chosen(column == head * NVAR + place // PP)


def same_head(columns):
    return chosen(down_rows((columns, columns)) // NVAR == across_lanes((columns, columns)) // NVAR)


def mover_of(ids_row):
    shape = (PIXEL_ROWS, NVAR)
    slot_ids = jnp.where(down_rows(shape) // PP == across_lanes(shape), ids_row, 0)
    wanted = jnp.sum(slot_ids, axis=1, keepdims=True)
    shape = (PIXEL_ROWS, PIXEL_ROWS)
    return chosen(wanted * PP + down_rows(shape) % PP == across_lanes(shape))


def pool_kernel(
    heads, facts_ref, ids_ref, pixels_ref, weight_ref, bias_ref, embed_ref, query_ref, in_ref, out_ref,
    part_ref, places_ref, w_ref, pooled_ref, keys_ref, values_ref, queries_ref, table_ref, folded_ref,
):
    columns, width = heads * NVAR, heads * HD
    dataset, live_count = facts_ref[0], facts_ref[1]
    ids_row = ids_ref[...]
    places = full(pixels_ref[...], mover_of(ids_row))
    places_ref[...] = places
    table_ref[:PIXEL_ROWS] = weight_ref[...]
    table_ref[PIXEL_ROWS:] = bias_ref[...] + embed_ref[...]
    table = table_ref[...]
    keys_ref[...] = full(table, in_ref[1])
    values_ref[...] = full(table, in_ref[2])
    queries = full(query_ref[...], in_ref[0])
    queries_ref[...] = queries
    query = jnp.sum(jnp.where(down_rows(queries.shape) == dataset, queries, 0.0), axis=0, keepdims=True)
    query = query * (1.0 / math.sqrt(HD))
    of_head = chosen(down_rows((width, columns)) // HD == across_lanes((width, columns)) // NVAR)
    keys = keys_ref[...] * query
    wide = full(keys, of_head)
    pixel_shape, offset_shape = (PIXEL_ROWS, columns), (NVAR, columns)
    pixel_scores = jnp.where(down_rows(pixel_shape) // PP == across_lanes(pixel_shape) % NVAR, wide[:PIXEL_ROWS], 0.0)
    offset_scores = jnp.where(down_rows(offset_shape) == across_lanes(offset_shape) % NVAR, wide[PIXEL_ROWS:], 0.0)
    scores = full(places, pixel_scores) + jnp.sum(offset_scores, axis=0, keepdims=True)
    square = (NVAR, NVAR)
    ids_down = jnp.sum(jnp.where(down_rows(square) == across_lanes(square), ids_row, 0), axis=1, keepdims=True)
    alive = (ids_down == across_lanes(offset_shape) % NVAR) & (down_rows(offset_shape) < live_count)
    live = jnp.sum(chosen(alive), axis=0, keepdims=True)
    scores = jnp.where(live > 0.5, scores, -1e30)
    head_at = across_lanes(scores.shape) // NVAR
    largest = jnp.zeros_like(scores)
    for h in range(heads):
        top = jnp.max(jnp.where(head_at == h, scores, -1e30), axis=1, keepdims=True)
        largest = jnp.where(head_at == h, top, largest)
    powers = jnp.exp(scores - largest)
    weights = powers / full(powers, same_head(columns))
    w_ref[...] = weights
    values = values_ref[...]
    offsets = full(holds_variable(heads), values[PIXEL_ROWS:])
    offsets = jnp.where(down_rows(offsets.shape) // NVAR == across_lanes(offsets.shape) // HD, offsets, 0.0)
    pooled = full(weights, offsets)
    for h in range(heads):
        mixed = full(weights, holds(PIXEL_ROWS, columns, h), ((1,), (1,))) * places
        part = full(mixed, values[:PIXEL_ROWS])
        pooled = pooled + jnp.where(across_lanes(part.shape) // HD == h, part, 0.0)
    pooled_ref[...] = pooled
    part_ref[...] = full(pooled, out_ref[...])
    rows = (8, width)
    by_head = jnp.where(across_lanes(rows) // HD == down_rows(rows), query, 0.0)
    folded_ref[...] = full(by_head, keys_ref[:PIXEL_ROWS], ((1,), (1,)))


def holds_variable(heads):
    shape = (heads * NVAR, NVAR)
    return chosen(down_rows(shape) % NVAR == across_lanes(shape))


def pool_back_kernel(
    heads, ids_ref, grad_ref, out_ref, places_ref, w_ref, values_ref, folded_ref,
    pixel_ref, value_raw_ref, score_raw_ref, offset_raw_ref,
):
    columns = heads * NVAR
    weights, places, values = w_ref[...], places_ref[...], values_ref[...]
    g_pool = full(grad_ref[...], out_ref[...], ((1,), (1,)))
    variable = holds_variable(heads)
    offsets = full(variable, values[PIXEL_ROWS:])
    own_head = down_rows(offsets.shape) // NVAR == across_lanes(offsets.shape) // HD
    g_pw = full(g_pool, jnp.where(own_head, offsets, 0.0), ((1,), (1,)))
    backs, mixes, g_heads = [], [], []
    for h in range(heads):
        g_head = jnp.where(across_lanes(g_pool.shape) // HD == h, g_pool, 0.0)
        back = full(g_head, values[:PIXEL_ROWS], ((1,), (1,)))
        holder = holds(PIXEL_ROWS, columns, h)
        g_pw = g_pw + full(places * back, holder)
        backs.append(back)
        g_heads.append(g_head)
    weighted = weights * g_pw
    g_ps = weighted - weights * full(weighted, same_head(columns))
    g_places = jnp.zeros_like(places)
    value_raw = jnp.zeros_like(values[:PIXEL_ROWS])
    score_raw_ref[...] = jnp.zeros_like(score_raw_ref)
    for h in range(heads):
        holder = holds(PIXEL_ROWS, columns, h)
        w_wide = full(weights, holder, ((1,), (1,)))
        g_wide = full(g_ps, holder, ((1,), (1,)))
        score_raw_ref[h : h + 1] = jnp.sum(places * g_wide, axis=0, keepdims=True)
        value_raw = value_raw + full(w_wide * places, g_heads[h], ((0,), (0,)))
        g_places = g_places + g_wide * folded_ref[h : h + 1] + w_wide * backs[h]
    value_raw_ref[:PIXEL_ROWS] = value_raw
    offset_values = jnp.where(own_head, full(weights, g_pool, ((0,), (0,))), 0.0)
    value_raw_ref[PIXEL_ROWS:] = full(variable, offset_values, ((0,), (0,)))
    rows = (8, columns)
    by_head = jnp.where(across_lanes(rows) // NVAR == down_rows(rows), jnp.sum(g_ps, axis=0, keepdims=True), 0.0)
    offset_raw_ref[...] = full(by_head, variable)
    pixel_ref[...] = full(g_places, mover_of(ids_ref[...]), ((1,), (1,)))


def in_vmem(kernel, name, outs, scalars, arrays, flops, limit):
    held = pl.BlockSpec(memory_space=pltpu.VMEM)
    return pl.pallas_call(
        kernel,
        out_shape=[jax.ShapeDtypeStruct(shape, jnp.float32) for shape in outs],
        in_specs=[pl.BlockSpec(memory_space=pltpu.SMEM)] * len(scalars) + [held] * len(arrays),
        out_specs=[held] * len(outs),
        compiler_params=pltpu.CompilerParams(vmem_limit_bytes=limit * 1024 * 1024),
        cost_estimate=pl.CostEstimate(flops=flops, bytes_accessed=sum(a.size for a in arrays) * 4, transcendentals=0),
        name=name,
    )(*scalars, *arrays)


def cut_kernel(block_ref, in_ref, out_ref, pool_ref):
    step = pl.program_id(0)
    block = block_ref[...]

    @pl.when(step < 3)
    def _():
        in_ref[...] = block

    @pl.when(step == 3)
    def _():
        out_ref[...] = block.T

    @pl.when(step == 4)
    def _():
        pool_ref[...] = block.T


def cut_apart(stacked):
    width, local = stacked.shape[0] // 5, stacked.shape[1]
    return pl.pallas_call(
        cut_kernel,
        grid=(5,),
        out_shape=[
            jax.ShapeDtypeStruct((3 * width, local), jnp.float32),
            jax.ShapeDtypeStruct((local, width), jnp.float32),
            jax.ShapeDtypeStruct((local, width), jnp.float32),
        ],
        in_specs=[pl.BlockSpec((width, local), lambda i: (i, 0))],
        out_specs=[
            pl.BlockSpec((width, local), lambda i: (jnp.minimum(i, 2), 0)),
            pl.BlockSpec((local, width), lambda i: (0, 0)),
            pl.BlockSpec((local, width), lambda i: (0, 0)),
        ],
        compiler_params=pltpu.CompilerParams(vmem_limit_bytes=24 * 1024 * 1024),
        cost_estimate=pl.CostEstimate(flops=0, bytes_accessed=8 * stacked.size, transcendentals=0),
        name="cut_apart",
    )(stacked)


def shards(
    pixels,
    variable_ids,
    variable_counts,
    lead_hours,
    dataset_ids,
    patch_counts,
    patch_weight,
    patch_bias,
    variable_embed,
    pool_query,
    pool_in,
    pool_out,
    position_embed,
    lead_weight,
    lead_bias,
    first_gain,
    first_shift,
    attention_in,
    attention_out,
    attention_bias,
    second_gain,
    second_shift,
    up_weight,
    up_bias,
    down_weight,
    down_bias,
    cotangent,
):
    direct = is_direct()
    length, width = cotangent.shape
    heads = pool_out.shape[0] // HD
    table_rows = NVAR * (PP + 1)
    key_live = jnp.arange(length) < patch_counts[0]
    row_mask = key_live.astype(jnp.float32)[:, None]
    lead_scale = lead_hours[0].astype(jnp.float32) / 168.0
    pick_set = (dataset_ids[0] == jnp.arange(NDATA)).astype(jnp.float32)
    grad_rows = cotangent * row_mask
    half_rows = length // 2
    grads_round = Round(rows_of(grad_rows, side(), half_rows))
    grads_came = grads_round.send()
    count = jnp.full((8, 128), patch_counts[0].astype(jnp.float32))

    def count_send(away):
        return dp_swap(count, away) if direct else 0.0

    if not direct:
        count = lax.psum(count, "dp")
    count_came = count_send(1)

    local = heads * HD
    columns = heads * NVAR
    facts = jnp.concatenate([dataset_ids, variable_counts]).astype(jnp.int32)
    query_rows = jnp.pad(pool_query, ((0, 8 - NDATA), (0, 0)))
    pool_part, places, pool_w, pooled, key_table, value_table, queries, table, folded = in_vmem(
        functools.partial(pool_kernel, heads),
        "pool",
        [
            (length, width), (length, PIXEL_ROWS), (length, columns), (length, local), (table_rows, local),
            (table_rows, local), (8, local), (table_rows, width), (8, PIXEL_ROWS),
        ],
        [facts],
        [
            variable_ids, pixels, patch_weight.reshape(PIXEL_ROWS, width), patch_bias, variable_embed, query_rows,
            pool_in, pool_out,
        ],
        10**9,
        40,
    )
    pool_part, grads_came = together(pool_part, grads_came)
    grads_round.land(grads_came)
    grads_came = grads_round.send()
    pool_sum = MpSum(pool_part)
    across = pool_sum.cross(pool_sum.start())
    across, grads_came, count_came = together(across, grads_came, count_came)
    count = count + count_came
    count_came = count_send(2)
    block_input = pool_sum.finish(across) + position_embed + lead_scale * lead_weight + lead_bias
    grads_round.land(grads_came)
    grads_came = grads_round.send()

    hat_one, inverse_one = normalise(block_input)
    norm_one = hat_one * first_gain + first_shift
    att_q, att_k, att_v = [mm(norm_one, attention_in[j]) for j in range(3)]

    def in_heads(array):
        return [array[:, h * HD : (h + 1) * HD] for h in range(heads)]

    q_heads, k_heads, v_heads = in_heads(att_q), in_heads(att_k), in_heads(att_v)
    att_w = []
    for h in range(heads):
        token_scores = mm_t(q_heads[h], k_heads[h]) / math.sqrt(HD)
        att_w.append(jax.nn.softmax(jnp.where(key_live[None, :], token_scores, -1e30), axis=1))
    attended = jnp.concatenate([mm(att_w[h], v_heads[h]) for h in range(heads)], axis=1)
    attention_sum = MpSum(mm(attended, attention_out))
    near, grads_came = together(attention_sum.start(), grads_came)
    across = attention_sum.cross(near)
    grads_round.land(grads_came)
    grads_came = grads_round.send()
    g_hidden = mm_t(grad_rows, down_weight)
    across, grads_came, count_came, g_hidden = together(across, grads_came, count_came, g_hidden)
    count = count + count_came
    count_came = count_send(4)
    middle = block_input + attention_sum.finish(across) + attention_bias
    grads_round.land(grads_came)

    hat_two, inverse_two = normalise(middle)
    norm_two = hat_two * second_gain + second_shift
    norm_round = Round(rows_of(norm_two, side(), half_rows))
    norm_came = norm_round.send()
    up_pre = mm(norm_two, up_weight) + up_bias
    hidden, slope = activate(up_pre)
    g_up = g_hidden * slope
    back_sum = MpSum(mm_t(g_up, up_weight))
    near, norm_came = together(back_sum.start(), norm_came)
    across = back_sum.cross(near)
    norm_round.land(norm_came)
    norm_came = norm_round.send()
    back_mine = grads_other = ()
    if direct:
        grads_mine = grads_round.merged()
        grads_other = mp_swap(grads_mine, 1)
        back_mine = mm_t(grads_mine, down_weight)
    across, norm_came, back_mine, count_came = together(across, norm_came, back_mine, count_came)
    scale = 1.0 / (count + count_came)[0, 0]
    g_n2 = back_sum.finish(across)
    norm_round.land(norm_came)
    norm_came = norm_round.send()
    g_middle = grad_rows + normalise_back(g_n2 * second_gain, hat_two, inverse_two)
    output_sum = MpSum(mm(hidden, down_weight))
    output_across = output_sum.cross(output_sum.start())

    g_att = in_heads(mm_t(g_middle, attention_out))
    g_q, g_k, g_v = [], [], []
    for h in range(heads):
        g_w = mm_t(g_att[h], v_heads[h])
        g_s = att_w[h] * (g_w - jnp.sum(att_w[h] * g_w, axis=1, keepdims=True)) / math.sqrt(HD)
        g_q.append(mm(g_s, k_heads[h]))
        g_k.append(t_mm(g_s, q_heads[h]))
        g_v.append(t_mm(att_w[h], g_att[h]))
    g_qkv = [jnp.concatenate(g, axis=1) for g in (g_q, g_k, g_v)]
    g_n1_part = mm_t(g_qkv[0], attention_in[0]) + mm_t(g_qkv[1], attention_in[1]) + mm_t(g_qkv[2], attention_in[2])
    input_sum = MpSum(g_n1_part)
    near, norm_came, output_across, g_later, attended = together(
        input_sum.start(), norm_came, output_across, g_qkv, attended
    )
    across = input_sum.cross(near)
    norm_round.land(norm_came)
    norm_came = norm_round.send()
    raw = [t_mm(norm_one, g * scale) for g in g_later] + [t_mm(g_middle, attended * scale)]
    raw = jnp.concatenate(raw + [jnp.zeros((width, heads * HD), jnp.float32)], axis=0)
    across, norm_came, raw = together(across, norm_came, raw)
    g_n1 = input_sum.finish(across)
    norm_round.land(norm_came)
    g_input = g_middle + normalise_back(g_n1 * first_gain, hat_one, inverse_one)

    pool_out_raw, g_input = together(t_mm(g_input, pooled * scale), g_input)
    raw = lax.dynamic_update_slice_in_dim(raw, pool_out_raw, 4 * width, 0)
    norm_pieces = norm_round.pieces if direct else ()
    raw, norm_pieces, grads_later = together(raw, norm_pieces, grads_other)
    raw_part = lax.psum_scatter(raw, "dp", scatter_dimension=0, tiled=True)
    pixel_part, value_raw, score_raw, offset_raw = in_vmem(
        functools.partial(pool_back_kernel, heads),
        "pool_back",
        [(length, PIXEL_ROWS), (table_rows, local), (8, PIXEL_ROWS), (8, NVAR)],
        [],
        [variable_ids, g_input, pool_out, places, pool_w, value_table, folded],
        10**9,
        40,
    )
    score_raw = jnp.concatenate([score_raw, offset_raw], axis=1)[:heads]
    score_raw = (pick_set[:, None, None] * score_raw[None]).reshape(NDATA * heads, table_rows)
    score_raw = jnp.pad(score_raw, ((0, 0), (0, local - table_rows)))
    lead_bias_raw = jnp.sum(g_input, axis=0)
    vectors = jnp.stack([
        lead_scale * lead_bias_raw,
        lead_bias_raw,
        jnp.sum(g_n1 * hat_one, axis=0),
        jnp.sum(g_n1, axis=0),
        jnp.sum(g_middle, axis=0),
        jnp.sum(g_n2 * hat_two, axis=0),
        jnp.sum(g_n2, axis=0),
        jnp.sum(g_up, axis=0),
        jnp.sum(grad_rows, axis=0),
    ])
    own = lax.axis_index("mp")
    quarter = length // lax.axis_size("mp")
    small = [value_raw, score_raw, vectors.reshape(-1, local)]
    used = sum(piece.shape[0] for piece in small)
    filler = jnp.zeros((-used % 8, local), jnp.float32)
    small = jnp.concatenate(small + [filler, rows_of(g_input, own, quarter).reshape(-1, local)], axis=0)

    def small_send(away):
        return dp_swap(small, away) if direct else 0.0

    if not direct:
        small = lax.psum(small, "dp")
    up_mine = up_other = down_sum = slope = up_sum = back_other = ()
    if direct:
        norm_round.pieces = norm_pieces
        norm_mine = norm_round.merged()
        norm_other = mp_swap(norm_mine, 1)
        up_mine = mm(norm_mine, up_weight)
        back_other = mm_t(grads_later, down_weight)
    small_came, up_mine, back_other, output_across = together(small_send(1), up_mine, back_other, output_across)
    block_output = (middle + output_sum.finish(output_across) + down_bias) * row_mask
    small = small + small_came
    if direct:
        hidden, slope = activate(up_mine + up_bias)
        down_sum = t_mm(hidden * scale, grads_mine)
    small_came, down_sum, slope = together(small_send(2), down_sum, slope)
    small = small + small_came
    small_came = small_send(4)
    if direct:
        up_sum = t_mm(norm_mine, back_mine * slope * scale)
        up_other = mm(norm_other, up_weight)
    small_came, up_sum, up_other, raw_part = together(small_came, up_sum, up_other, raw_part)
    raw_sum = lax.all_gather(raw_part, "dp", axis=0, tiled=True)
    small = (small + small_came) * scale
    value_sum = small[:table_rows]
    score_sum = small[table_rows : table_rows + NDATA * heads, :table_rows]
    vector_sums = small[table_rows + NDATA * heads : used].reshape(-1, width)
    position_sum = mp_gather(small[used + -used % 8 :].reshape(quarter, width))

    by_head = jnp.arange(local)[None, :] // HD == jnp.arange(NDATA * heads)[:, None] % heads
    by_head = by_head.astype(jnp.float32) / math.sqrt(HD)
    key_sum = t_mm(score_sum, by_head * jnp.repeat(queries[:NDATA], heads, axis=0))
    query_grad = jnp.sum((mm(score_sum, key_table) * by_head).reshape(NDATA, heads, local), axis=1)
    table_part = mm_t(key_sum, pool_in[1]) + mm_t(value_sum, pool_in[2])
    pool_query_part = mm_t(query_grad, pool_in[0])
    rest = length - (table_rows + NDATA)
    table_part = jnp.concatenate([table_part, pool_query_part, jnp.zeros((rest, width), jnp.float32)], axis=0)
    wide = jnp.concatenate([table_part, pixel_part], axis=1)
    table_sum = MpSum(wide)
    across = table_sum.cross(table_sum.start())
    if direct:
        hidden, slope = activate(up_other + up_bias)
        down_sum = down_sum + t_mm(hidden * scale, grads_other)
    across, down_sum, slope = together(across, down_sum, slope)
    sums = table_sum.finish(across)
    table_sums, pixels_grad = sums[:, :width], sums[:, width:]
    patch_weight_grad = table_sums[: NVAR * PP].reshape(NVAR, PP, width)
    offset_grad = table_sums[NVAR * PP : table_rows]
    pool_query_grad = table_sums[table_rows : table_rows + NDATA]
    lower = jnp.zeros((NDATA, value_sum.shape[1]), jnp.float32)
    upper = jnp.zeros((table_rows, value_sum.shape[1]), jnp.float32)
    pool_in_grad = lax.dot_general(
        jnp.stack([jnp.concatenate(pair, axis=0) for pair in ((upper, query_grad), (key_sum, lower), (value_sum, lower))]),
        jnp.concatenate([table, pool_query], axis=0),
        (((1,), (0,)), ((), ())),
        precision=exact,
    ).transpose(0, 2, 1)

    if direct:
        up_sum = up_sum + t_mm(norm_other, back_other * slope * scale)
    else:
        down_sum = lax.psum(t_mm(hidden, grad_rows), "dp") * scale
        up_sum = lax.psum(t_mm(norm_two, g_up), "dp") * scale
    raw_sum, up_sum = together(raw_sum, up_sum)
    attention_in_sum, attention_out_sum, pool_out_sum = cut_apart(raw_sum)
    return (
        block_output,
        pixels_grad,
        patch_weight_grad,
        offset_grad,
        offset_grad,
        pool_query_grad,
        pool_in_grad,
        pool_out_sum,
        position_sum,
        vector_sums[0],
        vector_sums[1],
        vector_sums[2],
        vector_sums[3],
        attention_in_sum.reshape(attention_in.shape),
        attention_out_sum,
        vector_sums[4],
        vector_sums[5],
        vector_sums[6],
        up_sum,
        vector_sums[7],
        down_sum,
        vector_sums[8],
    )


def solution(mesh):
    return jax.shard_map(
        shards,
        mesh=mesh,
        in_specs=(
            P("dp", None),
            P("dp", None),
            P("dp"),
            P("dp"),
            P("dp"),
            P("dp"),
            P(),
            P(),
            P(),
            P(),
            P(None, None, "mp"),
            P("mp", None),
            P(),
            P(),
            P(),
            P(),
            P(),
            P(None, None, "mp"),
            P("mp", None),
            P(),
            P(),
            P(),
            P(None, "mp"),
            P("mp"),
            P("mp", None),
            P(),
            P("dp", None),
        ),
        out_specs=(
            P("dp", None),
            P("dp", None),
            P(),
            P(),
            P(),
            P(),
            P(None, None, "mp"),
            P("mp", None),
            P(),
            P(),
            P(),
            P(),
            P(),
            P(None, None, "mp"),
            P("mp", None),
            P(),
            P(),
            P(),
            P(None, "mp"),
            P("mp"),
            P("mp", None),
            P(),
        ),
        check_vma=False,
    )
```

```python
import functools
import math

import jax
import jax.numpy as jnp
from jax import lax
from jax.experimental import pallas as pl
from jax.experimental.pallas import tpu as pltpu
from jax.sharding import PartitionSpec as P

HD = 64
NVAR = 48
PP = 4
NDATA = 2
GROUPS = 8
SPLITS = 4

exact = lax.Precision.HIGH


def dot(left, right, contract):
    return lax.dot_general(left, right, (contract, ((), ())), precision=exact, preferred_element_type=jnp.float32)


def mm(left, right):
    return dot(left, right, ((1,), (0,)))


def mm_t(left, right):
    return dot(left, right, ((1,), (1,)))


def t_mm(left, right):
    return dot(left, right, ((0,), (0,)))


def together(*values):
    return lax.optimization_barrier(values)


def rows_of(array, place, count):
    return lax.dynamic_slice_in_dim(array, place * count, count)


def is_direct():
    return lax.axis_size("dp") == GROUPS and lax.axis_size("mp") == SPLITS


def dp_swap(array, away):
    return lax.ppermute(array, "dp", [(i, i ^ away) for i in range(GROUPS)])


def mp_swap(array, away):
    return lax.ppermute(array, "mp", [(i, i ^ away) for i in range(SPLITS)])


def lay_kernel(starts_ref, *refs):
    pieces, merged, sems = refs[:-2], refs[-2], refs[-1]
    copies = []
    for k, piece in enumerate(pieces):
        rows = piece.shape[0]
        target = merged.at[pl.ds(pl.multiple_of(starts_ref[k], rows), rows), :]
        copies.append(pltpu.make_async_copy(piece, target, sems.at[k]))
    for copy in copies:
        copy.start()
    for copy in copies:
        copy.wait()


def lay_together(starts, pieces, total_rows):
    shape = (total_rows,) + pieces[0].shape[1:]
    return pl.pallas_call(
        lay_kernel,
        out_shape=jax.ShapeDtypeStruct(shape, pieces[0].dtype),
        in_specs=[pl.BlockSpec(memory_space=pltpu.SMEM)] + [pl.BlockSpec(memory_space=pl.ANY)] * len(pieces),
        out_specs=pl.BlockSpec(memory_space=pltpu.VMEM),
        scratch_shapes=[pltpu.SemaphoreType.DMA((len(pieces),))],
        compiler_params=pltpu.CompilerParams(vmem_limit_bytes=16 * 1024 * 1024),
        cost_estimate=pl.CostEstimate(flops=0, bytes_accessed=2 * math.prod(shape) * 4, transcendentals=0),
        name="lay_together",
    )(jnp.stack(starts).astype(jnp.int32), *pieces)


class Round:
    def __init__(self, rows):
        self.direct, self.count = is_direct(), rows.shape[0]
        if not self.direct:
            return
        order = [i for i in range(0, GROUPS, 2)] + [i for i in reversed(range(1, GROUPS, 2))]
        self.right = [(order[i], order[(i + 1) % GROUPS]) for i in range(GROUPS)]
        self.left = [(b, a) for a, b in self.right]
        own = lax.axis_index("dp")
        self.place = jnp.where(own % 2 == 0, own // 2, GROUPS - 1 - own // 2)
        self.step, self.held = 0, (rows, rows)
        self.pieces, self.starts = [rows], [self.place * self.count]

    def send(self):
        if not self.direct:
            return ()
        self.step += 1
        one, two = self.held
        if self.step == GROUPS // 2:
            one, two = one[: self.count // 2], two[self.count // 2 :]
        return lax.ppermute(one, "dp", self.right), lax.ppermute(two, "dp", self.left)

    def land(self, came):
        if not self.direct:
            return
        self.held = came
        skip = self.count // 2 if self.step == GROUPS // 2 else 0
        self.pieces += list(came)
        for away, more in ((-self.step, 0), (self.step, skip)):
            self.starts.append(lax.rem(self.place + (away + GROUPS), GROUPS) * self.count + more)

    def merged(self):
        return lay_together(self.starts, self.pieces, GROUPS * self.count)


def side():
    return lax.axis_index("mp") % 2


class MpSum:
    def __init__(self, array):
        self.held, self.direct = array, is_direct()

    def start(self):
        if not self.direct:
            return lax.psum(self.held, "mp")
        return mp_swap(rows_of(self.held, 1 - side(), self.held.shape[0] // 2), 1)

    def cross(self, came):
        if not self.direct:
            self.held = came
            return ()
        self.held = rows_of(self.held, side(), self.held.shape[0] // 2) + came
        return mp_swap(self.held, 2)

    def finish(self, came):
        if not self.direct:
            return self.held
        mine = self.held + came
        other = mp_swap(mine, 1)
        first = side() == 0
        return jnp.concatenate([jnp.where(first, mine, other), jnp.where(first, other, mine)], axis=0)


def mp_gather(array):
    if not is_direct():
        return lax.all_gather(array, "mp", axis=0, tiled=True)
    own = lax.axis_index("mp")
    rows = array.shape[0]
    far = mp_swap(array, 2)
    near = mp_swap(jnp.concatenate([array, far], axis=0), 1)
    pieces = [array, far, near[:rows], near[rows:]]
    return lay_together([(own ^ k) * rows for k in (0, 2, 1, 3)], pieces, SPLITS * rows)


def normalise(values):
    centred = values - jnp.mean(values, axis=-1, keepdims=True)
    inverse = lax.rsqrt(jnp.mean(centred * centred, axis=-1, keepdims=True) + 1e-06)
    return centred * inverse, inverse


def activate(values):
    phi_sum = 0.5 * (1.0 + lax.erf(values * math.sqrt(0.5)))
    phi = jnp.exp(-0.5 * values * values) * (1.0 / math.sqrt(2.0 * math.pi))
    return values * phi_sum, phi_sum + values * phi


def normalise_back(grad, hat, inverse):
    return (grad - jnp.mean(grad, axis=-1, keepdims=True) - hat * jnp.mean(grad * hat, axis=-1, keepdims=True)) * inverse


def full(left, right, contract=((1,), (0,))):
    return lax.dot_general(
        left, right, (contract, ((), ())), precision=lax.Precision.HIGHEST, preferred_element_type=jnp.float32
    )


def across_lanes(shape):
    return lax.broadcasted_iota(jnp.int32, shape, len(shape) - 1)


def down_rows(shape):
    return lax.broadcasted_iota(jnp.int32, shape, 0)


def chosen(condition):
    return jnp.where(condition, 1.0, 0.0).astype(jnp.float32)


PIXEL_ROWS = NVAR * PP


def holds(rows, columns, head):
    place, column = down_rows((rows, columns)), across_lanes((rows, columns))
    return chosen(column == head * NVAR + place // PP)


def same_head(columns):
    return chosen(down_rows((columns, columns)) // NVAR == across_lanes((columns, columns)) // NVAR)


def mover_of(ids_row):
    shape = (PIXEL_ROWS, NVAR)
    slot_ids = jnp.where(down_rows(shape) // PP == across_lanes(shape), ids_row, 0)
    wanted = jnp.sum(slot_ids, axis=1, keepdims=True)
    shape = (PIXEL_ROWS, PIXEL_ROWS)
    return chosen(wanted * PP + down_rows(shape) % PP == across_lanes(shape))


def pool_kernel(
    heads, facts_ref, ids_ref, pixels_ref, weight_ref, bias_ref, embed_ref, query_ref, in_ref, out_ref,
    part_ref, places_ref, w_ref, pooled_ref, keys_ref, values_ref, queries_ref, table_ref, folded_ref,
):
    columns, width = heads * NVAR, heads * HD
    dataset, live_count = facts_ref[0], facts_ref[1]
    ids_row = ids_ref[...]
    places = full(pixels_ref[...], mover_of(ids_row))
    places_ref[...] = places
    table_ref[:PIXEL_ROWS] = weight_ref[...]
    table_ref[PIXEL_ROWS:] = bias_ref[...] + embed_ref[...]
    table = table_ref[...]
    keys_ref[...] = full(table, in_ref[1])
    values_ref[...] = full(table, in_ref[2])
    queries = full(query_ref[...], in_ref[0])
    queries_ref[...] = queries
    query = jnp.sum(jnp.where(down_rows(queries.shape) == dataset, queries, 0.0), axis=0, keepdims=True)
    query = query * (1.0 / math.sqrt(HD))
    of_head = chosen(down_rows((width, columns)) // HD == across_lanes((width, columns)) // NVAR)
    keys = keys_ref[...] * query
    wide = full(keys, of_head)
    pixel_shape, offset_shape = (PIXEL_ROWS, columns), (NVAR, columns)
    pixel_scores = jnp.where(down_rows(pixel_shape) // PP == across_lanes(pixel_shape) % NVAR, wide[:PIXEL_ROWS], 0.0)
    offset_scores = jnp.where(down_rows(offset_shape) == across_lanes(offset_shape) % NVAR, wide[PIXEL_ROWS:], 0.0)
    scores = full(places, pixel_scores) + jnp.sum(offset_scores, axis=0, keepdims=True)
    square = (NVAR, NVAR)
    ids_down = jnp.sum(jnp.where(down_rows(square) == across_lanes(square), ids_row, 0), axis=1, keepdims=True)
    alive = (ids_down == across_lanes(offset_shape) % NVAR) & (down_rows(offset_shape) < live_count)
    live = jnp.sum(chosen(alive), axis=0, keepdims=True)
    scores = jnp.where(live > 0.5, scores, -1e30)
    head_at = across_lanes(scores.shape) // NVAR
    largest = jnp.zeros_like(scores)
    for h in range(heads):
        top = jnp.max(jnp.where(head_at == h, scores, -1e30), axis=1, keepdims=True)
        largest = jnp.where(head_at == h, top, largest)
    powers = jnp.exp(scores - largest)
    weights = powers / full(powers, same_head(columns))
    w_ref[...] = weights
    values = values_ref[...]
    offsets = full(holds_variable(heads), values[PIXEL_ROWS:])
    offsets = jnp.where(down_rows(offsets.shape) // NVAR == across_lanes(offsets.shape) // HD, offsets, 0.0)
    pooled = full(weights, offsets)
    for h in range(heads):
        mixed = full(weights, holds(PIXEL_ROWS, columns, h), ((1,), (1,))) * places
        part = full(mixed, values[:PIXEL_ROWS])
        pooled = pooled + jnp.where(across_lanes(part.shape) // HD == h, part, 0.0)
    pooled_ref[...] = pooled
    part_ref[...] = full(pooled, out_ref[...])
    rows = (8, width)
    by_head = jnp.where(across_lanes(rows) // HD == down_rows(rows), query, 0.0)
    folded_ref[...] = full(by_head, keys_ref[:PIXEL_ROWS], ((1,), (1,)))


def holds_variable(heads):
    shape = (heads * NVAR, NVAR)
    return chosen(down_rows(shape) % NVAR == across_lanes(shape))


def pool_back_kernel(
    heads, ids_ref, grad_ref, out_ref, places_ref, w_ref, values_ref, folded_ref,
    pixel_ref, value_raw_ref, score_raw_ref, offset_raw_ref,
):
    columns = heads * NVAR
    weights, places, values = w_ref[...], places_ref[...], values_ref[...]
    g_pool = full(grad_ref[...], out_ref[...], ((1,), (1,)))
    variable = holds_variable(heads)
    offsets = full(variable, values[PIXEL_ROWS:])
    own_head = down_rows(offsets.shape) // NVAR == across_lanes(offsets.shape) // HD
    g_pw = full(g_pool, jnp.where(own_head, offsets, 0.0), ((1,), (1,)))
    backs, mixes, g_heads = [], [], []
    for h in range(heads):
        g_head = jnp.where(across_lanes(g_pool.shape) // HD == h, g_pool, 0.0)
        back = full(g_head, values[:PIXEL_ROWS], ((1,), (1,)))
        holder = holds(PIXEL_ROWS, columns, h)
        g_pw = g_pw + full(places * back, holder)
        backs.append(back)
        g_heads.append(g_head)
    weighted = weights * g_pw
    g_ps = weighted - weights * full(weighted, same_head(columns))
    g_places = jnp.zeros_like(places)
    value_raw = jnp.zeros_like(values[:PIXEL_ROWS])
    score_raw_ref[...] = jnp.zeros_like(score_raw_ref)
    for h in range(heads):
        holder = holds(PIXEL_ROWS, columns, h)
        w_wide = full(weights, holder, ((1,), (1,)))
        g_wide = full(g_ps, holder, ((1,), (1,)))
        score_raw_ref[h : h + 1] = jnp.sum(places * g_wide, axis=0, keepdims=True)
        value_raw = value_raw + full(w_wide * places, g_heads[h], ((0,), (0,)))
        g_places = g_places + g_wide * folded_ref[h : h + 1] + w_wide * backs[h]
    value_raw_ref[:PIXEL_ROWS] = value_raw
    offset_values = jnp.where(own_head, full(weights, g_pool, ((0,), (0,))), 0.0)
    value_raw_ref[PIXEL_ROWS:] = full(variable, offset_values, ((0,), (0,)))
    rows = (8, columns)
    by_head = jnp.where(across_lanes(rows) // NVAR == down_rows(rows), jnp.sum(g_ps, axis=0, keepdims=True), 0.0)
    offset_raw_ref[...] = full(by_head, variable)
    pixel_ref[...] = full(g_places, mover_of(ids_ref[...]), ((1,), (1,)))


def in_vmem(kernel, name, outs, scalars, arrays, flops, limit):
    held = pl.BlockSpec(memory_space=pltpu.VMEM)
    return pl.pallas_call(
        kernel,
        out_shape=[jax.ShapeDtypeStruct(shape, jnp.float32) for shape in outs],
        in_specs=[pl.BlockSpec(memory_space=pltpu.SMEM)] * len(scalars) + [held] * len(arrays),
        out_specs=[held] * len(outs),
        compiler_params=pltpu.CompilerParams(vmem_limit_bytes=limit * 1024 * 1024),
        cost_estimate=pl.CostEstimate(flops=flops, bytes_accessed=sum(a.size for a in arrays) * 4, transcendentals=0),
        name=name,
    )(*scalars, *arrays)


def cut_kernel(block_ref, in_ref, out_ref, pool_ref):
    step = pl.program_id(0)
    block = block_ref[...]

    @pl.when(step < 3)
    def _():
        in_ref[...] = block

    @pl.when(step == 3)
    def _():
        out_ref[...] = block.T

    @pl.when(step == 4)
    def _():
        pool_ref[...] = block.T


def cut_apart(stacked):
    width, local = stacked.shape[0] // 5, stacked.shape[1]
    return pl.pallas_call(
        cut_kernel,
        grid=(5,),
        out_shape=[
            jax.ShapeDtypeStruct((3 * width, local), jnp.float32),
            jax.ShapeDtypeStruct((local, width), jnp.float32),
            jax.ShapeDtypeStruct((local, width), jnp.float32),
        ],
        in_specs=[pl.BlockSpec((width, local), lambda i: (i, 0))],
        out_specs=[
            pl.BlockSpec((width, local), lambda i: (jnp.minimum(i, 2), 0)),
            pl.BlockSpec((local, width), lambda i: (0, 0)),
            pl.BlockSpec((local, width), lambda i: (0, 0)),
        ],
        compiler_params=pltpu.CompilerParams(vmem_limit_bytes=24 * 1024 * 1024),
        cost_estimate=pl.CostEstimate(flops=0, bytes_accessed=8 * stacked.size, transcendentals=0),
        name="cut_apart",
    )(stacked)


def shards(
    pixels,
    variable_ids,
    variable_counts,
    lead_hours,
    dataset_ids,
    patch_counts,
    patch_weight,
    patch_bias,
    variable_embed,
    pool_query,
    pool_in,
    pool_out,
    position_embed,
    lead_weight,
    lead_bias,
    first_gain,
    first_shift,
    attention_in,
    attention_out,
    attention_bias,
    second_gain,
    second_shift,
    up_weight,
    up_bias,
    down_weight,
    down_bias,
    cotangent,
):
    direct = is_direct()
    length, width = cotangent.shape
    heads = pool_out.shape[0] // HD
    table_rows = NVAR * (PP + 1)
    key_live = jnp.arange(length) < patch_counts[0]
    row_mask = key_live.astype(jnp.float32)[:, None]
    lead_scale = lead_hours[0].astype(jnp.float32) / 168.0
    pick_set = (dataset_ids[0] == jnp.arange(NDATA)).astype(jnp.float32)
    grad_rows = cotangent * row_mask
    half_rows = length // 2
    grads_round = Round(rows_of(grad_rows, side(), half_rows))
    grads_came = grads_round.send()
    count = jnp.full((8, 128), patch_counts[0].astype(jnp.float32))

    def count_send(away):
        return dp_swap(count, away) if direct else 0.0

    if not direct:
        count = lax.psum(count, "dp")
    count_came = count_send(1)

    local = heads * HD
    columns = heads * NVAR
    facts = jnp.concatenate([dataset_ids, variable_counts]).astype(jnp.int32)
    query_rows = jnp.pad(pool_query, ((0, 8 - NDATA), (0, 0)))
    pool_part, places, pool_w, pooled, key_table, value_table, queries, table, folded = in_vmem(
        functools.partial(pool_kernel, heads),
        "pool",
        [
            (length, width), (length, PIXEL_ROWS), (length, columns), (length, local), (table_rows, local),
            (table_rows, local), (8, local), (table_rows, width), (8, PIXEL_ROWS),
        ],
        [facts],
        [
            variable_ids, pixels, patch_weight.reshape(PIXEL_ROWS, width), patch_bias, variable_embed, query_rows,
            pool_in, pool_out,
        ],
        10**9,
        40,
    )
    pool_part, grads_came = together(pool_part, grads_came)
    grads_round.land(grads_came)
    grads_came = grads_round.send()
    pool_sum = MpSum(pool_part)
    across = pool_sum.cross(pool_sum.start())
    across, grads_came, count_came = together(across, grads_came, count_came)
    count = count + count_came
    count_came = count_send(2)
    block_input = pool_sum.finish(across) + position_embed + lead_scale * lead_weight + lead_bias
    grads_round.land(grads_came)
    grads_came = grads_round.send()

    hat_one, inverse_one = normalise(block_input)
    norm_one = hat_one * first_gain + first_shift
    att_q, att_k, att_v = [mm(norm_one, attention_in[j]) for j in range(3)]

    def in_heads(array):
        return [array[:, h * HD : (h + 1) * HD] for h in range(heads)]

    q_heads, k_heads, v_heads = in_heads(att_q), in_heads(att_k), in_heads(att_v)
    att_w = []
    for h in range(heads):
        token_scores = mm_t(q_heads[h], k_heads[h]) / math.sqrt(HD)
        att_w.append(jax.nn.softmax(jnp.where(key_live[None, :], token_scores, -1e30), axis=1))
    attended = jnp.concatenate([mm(att_w[h], v_heads[h]) for h in range(heads)], axis=1)
    attention_sum = MpSum(mm(attended, attention_out))
    near, grads_came = together(attention_sum.start(), grads_came)
    across = attention_sum.cross(near)
    grads_round.land(grads_came)
    grads_came = grads_round.send()
    g_hidden = mm_t(grad_rows, down_weight)
    across, grads_came, count_came, g_hidden = together(across, grads_came, count_came, g_hidden)
    count = count + count_came
    count_came = count_send(4)
    middle = block_input + attention_sum.finish(across) + attention_bias
    grads_round.land(grads_came)

    hat_two, inverse_two = normalise(middle)
    norm_two = hat_two * second_gain + second_shift
    norm_round = Round(rows_of(norm_two, side(), half_rows))
    norm_came = norm_round.send()
    up_pre = mm(norm_two, up_weight) + up_bias
    hidden, slope = activate(up_pre)
    g_up = g_hidden * slope
    back_sum = MpSum(mm_t(g_up, up_weight))
    near, norm_came = together(back_sum.start(), norm_came)
    across = back_sum.cross(near)
    norm_round.land(norm_came)
    norm_came = norm_round.send()
    grads_mine = grads_other = ()
    if direct:
        grads_mine = grads_round.merged()
        grads_other = mp_swap(grads_mine, 1)
    across, norm_came, count_came = together(across, norm_came, count_came)
    scale = 1.0 / (count + count_came)[0, 0]
    g_n2 = back_sum.finish(across)
    norm_round.land(norm_came)
    norm_came = norm_round.send()
    g_middle = grad_rows + normalise_back(g_n2 * second_gain, hat_two, inverse_two)
    output_sum = MpSum(mm(hidden, down_weight))
    output_across = output_sum.cross(output_sum.start())

    g_att = in_heads(mm_t(g_middle, attention_out))
    g_q, g_k, g_v = [], [], []
    for h in range(heads):
        g_w = mm_t(g_att[h], v_heads[h])
        g_s = att_w[h] * (g_w - jnp.sum(att_w[h] * g_w, axis=1, keepdims=True)) / math.sqrt(HD)
        g_q.append(mm(g_s, k_heads[h]))
        g_k.append(t_mm(g_s, q_heads[h]))
        g_v.append(t_mm(att_w[h], g_att[h]))
    g_qkv = [jnp.concatenate(g, axis=1) for g in (g_q, g_k, g_v)]
    g_n1_part = mm_t(g_qkv[0], attention_in[0]) + mm_t(g_qkv[1], attention_in[1]) + mm_t(g_qkv[2], attention_in[2])
    input_sum = MpSum(g_n1_part)
    near, norm_came, output_across, g_later, attended = together(
        input_sum.start(), norm_came, output_across, g_qkv, attended
    )
    across = input_sum.cross(near)
    norm_round.land(norm_came)
    norm_came = norm_round.send()
    raw = [t_mm(norm_one, g * scale) for g in g_later] + [t_mm(g_middle, attended * scale)]
    raw = jnp.concatenate(raw + [jnp.zeros((width, heads * HD), jnp.float32)], axis=0)
    across, norm_came, raw = together(across, norm_came, raw)
    g_n1 = input_sum.finish(across)
    norm_round.land(norm_came)
    g_input = g_middle + normalise_back(g_n1 * first_gain, hat_one, inverse_one)

    pool_out_raw, g_input = together(t_mm(g_input, pooled * scale), g_input)
    raw = lax.dynamic_update_slice_in_dim(raw, pool_out_raw, 4 * width, 0)
    norm_pieces = norm_round.pieces if direct else ()
    raw, norm_pieces, grads_later, grads_mine = together(raw, norm_pieces, grads_other, grads_mine)
    raw_part = lax.psum_scatter(raw, "dp", scatter_dimension=0, tiled=True)
    pixel_part, value_raw, score_raw, offset_raw = in_vmem(
        functools.partial(pool_back_kernel, heads),
        "pool_back",
        [(length, PIXEL_ROWS), (table_rows, local), (8, PIXEL_ROWS), (8, NVAR)],
        [],
        [variable_ids, g_input, pool_out, places, pool_w, value_table, folded],
        10**9,
        40,
    )
    score_raw = jnp.concatenate([score_raw, offset_raw], axis=1)[:heads]
    score_raw = (pick_set[:, None, None] * score_raw[None]).reshape(NDATA * heads, table_rows)
    score_raw = jnp.pad(score_raw, ((0, 0), (0, local - table_rows)))
    lead_bias_raw = jnp.sum(g_input, axis=0)
    vectors = jnp.stack([
        lead_scale * lead_bias_raw,
        lead_bias_raw,
        jnp.sum(g_n1 * hat_one, axis=0),
        jnp.sum(g_n1, axis=0),
        jnp.sum(g_middle, axis=0),
        jnp.sum(g_n2 * hat_two, axis=0),
        jnp.sum(g_n2, axis=0),
        jnp.sum(g_up, axis=0),
        jnp.sum(grad_rows, axis=0),
    ])
    own = lax.axis_index("mp")
    quarter = length // lax.axis_size("mp")
    small = [value_raw, score_raw, vectors.reshape(-1, local)]
    used = sum(piece.shape[0] for piece in small)
    filler = jnp.zeros((-used % 8, local), jnp.float32)
    small = jnp.concatenate(small + [filler, rows_of(g_input, own, quarter).reshape(-1, local)], axis=0)

    def small_send(away):
        return dp_swap(small, away) if direct else 0.0

    if not direct:
        small = lax.psum(small, "dp")
    up_mine = up_other = down_sum = slope = up_sum = back_other = ()
    if direct:
        norm_round.pieces = norm_pieces
        norm_mine = norm_round.merged()
        norm_other = mp_swap(norm_mine, 1)
        up_mine = mm(norm_mine, up_weight)
        back_other = mm_t(grads_later, down_weight)
    small_came, up_mine, back_other, output_across = together(small_send(1), up_mine, back_other, output_across)
    block_output = (middle + output_sum.finish(output_across) + down_bias) * row_mask
    small = small + small_came
    if direct:
        hidden, slope = activate(up_mine + up_bias)
        down_sum = t_mm(hidden * scale, grads_mine)
        back_mine = mm_t(grads_mine, down_weight)
    small_came, down_sum, slope = together(small_send(2), down_sum, slope)
    small = small + small_came
    small_came = small_send(4)
    if direct:
        up_sum = t_mm(norm_mine, back_mine * slope * scale)
        up_other = mm(norm_other, up_weight)
    small_came, up_sum, up_other, raw_part = together(small_came, up_sum, up_other, raw_part)
    raw_sum = lax.all_gather(raw_part, "dp", axis=0, tiled=True)
    small = (small + small_came) * scale
    value_sum = small[:table_rows]
    score_sum = small[table_rows : table_rows + NDATA * heads, :table_rows]
    vector_sums = small[table_rows + NDATA * heads : used].reshape(-1, width)
    position_sum = mp_gather(small[used + -used % 8 :].reshape(quarter, width))

    by_head = jnp.arange(local)[None, :] // HD == jnp.arange(NDATA * heads)[:, None] % heads
    by_head = by_head.astype(jnp.float32) / math.sqrt(HD)
    key_sum = t_mm(score_sum, by_head * jnp.repeat(queries[:NDATA], heads, axis=0))
    query_grad = jnp.sum((mm(score_sum, key_table) * by_head).reshape(NDATA, heads, local), axis=1)
    table_part = mm_t(key_sum, pool_in[1]) + mm_t(value_sum, pool_in[2])
    pool_query_part = mm_t(query_grad, pool_in[0])
    rest = length - (table_rows + NDATA)
    table_part = jnp.concatenate([table_part, pool_query_part, jnp.zeros((rest, width), jnp.float32)], axis=0)
    wide = jnp.concatenate([table_part, pixel_part], axis=1)
    table_sum = MpSum(wide)
    across = table_sum.cross(table_sum.start())
    if direct:
        hidden, slope = activate(up_other + up_bias)
        down_sum = down_sum + t_mm(hidden * scale, grads_other)
    across, down_sum, slope = together(across, down_sum, slope)
    sums = table_sum.finish(across)
    table_sums, pixels_grad = sums[:, :width], sums[:, width:]
    patch_weight_grad = table_sums[: NVAR * PP].reshape(NVAR, PP, width)
    offset_grad = table_sums[NVAR * PP : table_rows]
    pool_query_grad = table_sums[table_rows : table_rows + NDATA]
    lower = jnp.zeros((NDATA, value_sum.shape[1]), jnp.float32)
    upper = jnp.zeros((table_rows, value_sum.shape[1]), jnp.float32)
    pool_in_grad = lax.dot_general(
        jnp.stack([jnp.concatenate(pair, axis=0) for pair in ((upper, query_grad), (key_sum, lower), (value_sum, lower))]),
        jnp.concatenate([table, pool_query], axis=0),
        (((1,), (0,)), ((), ())),
        precision=exact,
    ).transpose(0, 2, 1)

    if direct:
        up_sum = up_sum + t_mm(norm_other, back_other * slope * scale)
    else:
        down_sum = lax.psum(t_mm(hidden, grad_rows), "dp") * scale
        up_sum = lax.psum(t_mm(norm_two, g_up), "dp") * scale
    raw_sum, up_sum = together(raw_sum, up_sum)
    attention_in_sum, attention_out_sum, pool_out_sum = cut_apart(raw_sum)
    return (
        block_output,
        pixels_grad,
        patch_weight_grad,
        offset_grad,
        offset_grad,
        pool_query_grad,
        pool_in_grad,
        pool_out_sum,
        position_sum,
        vector_sums[0],
        vector_sums[1],
        vector_sums[2],
        vector_sums[3],
        attention_in_sum.reshape(attention_in.shape),
        attention_out_sum,
        vector_sums[4],
        vector_sums[5],
        vector_sums[6],
        up_sum,
        vector_sums[7],
        down_sum,
        vector_sums[8],
    )


def solution(mesh):
    return jax.shard_map(
        shards,
        mesh=mesh,
        in_specs=(
            P("dp", None),
            P("dp", None),
            P("dp"),
            P("dp"),
            P("dp"),
            P("dp"),
            P(),
            P(),
            P(),
            P(),
            P(None, None, "mp"),
            P("mp", None),
            P(),
            P(),
            P(),
            P(),
            P(),
            P(None, None, "mp"),
            P("mp", None),
            P(),
            P(),
            P(),
            P(None, "mp"),
            P("mp"),
            P("mp", None),
            P(),
            P("dp", None),
        ),
        out_specs=(
            P("dp", None),
            P("dp", None),
            P(),
            P(),
            P(),
            P(),
            P(None, None, "mp"),
            P("mp", None),
            P(),
            P(),
            P(),
            P(),
            P(),
            P(None, None, "mp"),
            P("mp", None),
            P(),
            P(),
            P(),
            P(None, "mp"),
            P("mp"),
            P("mp", None),
            P(),
        ),
        check_vma=False,
    )
```
